128 devices in a mesh: lat: 8 (over z, core), lon: 16 (over x, y).
Axes of the slice: x: 4, y: 4, z: 4, core: 2. Of those that a mesh axis runs over, the one named last changes fastest.
Arguments:
- grid_latent: bfloat16 [64, 2048, 512], P('lat', 'lon'), may hold values from -6 to 6
- mesh_latent: bfloat16 [8, 16, 320, 512], P('lat', 'lon'), may hold values from -6 to 6
- edge_latent: bfloat16 [8, 16, 2560, 512], P('lat', 'lon'), may hold values from -6 to 6
- g2m_src: int32 [8, 16, 1536], P('lat', 'lon'), may hold values from 0 to 1583, as said below
- g2m_dst: int32 [8, 16, 1536], P('lat', 'lon'), may hold values from 0 to 319
- g2m_count: int32 [8, 16], P('lat', 'lon'), may hold values from 577 to 1536, as said below
- mesh_src: int32 [8, 16, 2560], P('lat', 'lon'), may hold values from 0 to 4927, as said below
- mesh_dst: int32 [8, 16, 2560], P('lat', 'lon'), may hold values from 0 to 319
- m2g_src: int32 [3, 64, 2048], P(None, 'lat', 'lon'), may hold values from 0 to 2879, as said below
- weights_in: bfloat16 [18, 512, 512], replicated, may hold values from -0.25 to 0.25
- weights_out: bfloat16 [8, 512, 512], replicated, may hold values from -0.25 to 0.25
- gains: float32 [8, 512], replicated, may hold values from 0.25 to 1.75
Outputs:
- grid_out: bfloat16 [64, 2048, 512], P('lat', 'lon')
The draws below stay inside these ranges and needn't reach their ends.
Inputs may be any that keep to these rules, and one draw needn't show every extreme that they name: `g2m_src`: live slots read only cells of the widened tile that lie inside the latitude range of the grid (no cell beyond a pole). `g2m_count`: the first and last latitude bands fill all 1536 slots. `mesh_src`: A sender below 2880 is node j of nine-patch block k (index k * 320 + j); for k other than 4 the block lies inside the latitude range and j < 64. A sender of 2880 or more is a coarse node: the last 16 nodes of every patch in patch order. `m2g_src`: index k * 320 + j into the nine patches around the cell's tile; for k other than 4 the patch lies inside the latitude range and j < 64.
All inputs are finite; a program needn't handle non-finite values.
Results may differ from the reference program's by a relative error of at most 0.017.
Values may be sent and summed in bfloat16 or wider, within the bound.
A program may use at most 128 MiB of HBM per device.

```python
import jax
import jax.numpy as jnp
from jax import lax

L = 512
ROWS = 8
COLS = 128
HALO = 2
MESH = 320
BORDER = 64
COARSE = 16
EDGE = 2560
G2M = 1536
ROUNDS = 2
NROWS = 64
NCOLS = 2048
N_LAT = 8
N_LON = 16


def neighbour_block(key, lat_index, shape):
    first_key, second_key = jax.random.split(key)
    lat_step = jax.random.randint(first_key, shape, -1, 2)
    outside = (lat_index + lat_step < 0) | (lat_index + lat_step > N_LAT - 1)
    lat_step = jnp.where(outside, -lat_step, lat_step)
    lon_step = jax.random.randint(second_key, shape, -1, 2)
    lon_step = jnp.where((lat_step == 0) & (lon_step == 0), 1, lon_step)
    return (lat_step + 1) * 3 + lon_step + 1


def draw_g2m_src(key, part):
    key = jax.random.fold_in(key, 11)
    first_key, second_key = jax.random.split(key)
    shape = (N_LAT, N_LON, G2M)
    lat_index = jnp.arange(N_LAT, dtype=jnp.int32)[:, None, None]
    lowest = jnp.where(lat_index == 0, HALO, 0)
    highest = jnp.where(lat_index == N_LAT - 1, ROWS + HALO, ROWS + 2 * HALO)
    row_pick = lowest + jax.random.randint(first_key, shape, 0, 1 << 20) % (highest - lowest)
    col_pick = jax.random.randint(second_key, shape, 0, COLS + 2 * HALO)
    return (row_pick * (COLS + 2 * HALO) + col_pick).astype(jnp.int32)


def draw_g2m_dst(key, part):
    key = jax.random.fold_in(key, 12)
    return jax.random.randint(key, (N_LAT, N_LON, G2M), 0, MESH).astype(jnp.int32)


def draw_g2m_count(key, part):
    key = jax.random.fold_in(key, 13)
    lat_index = jnp.arange(N_LAT, dtype=jnp.int32)[:, None]
    distance = jnp.abs(2 * lat_index - (N_LAT - 1))
    polar = (lat_index == 0) | (lat_index == N_LAT - 1)
    base_count = G2M - G2M // 2 * (N_LAT - 1 - distance) // (N_LAT - 1)
    jitter = jax.random.randint(key, (N_LAT, N_LON), 0, G2M // 8)
    return jnp.where(polar, G2M, base_count - jitter).astype(jnp.int32)


def draw_mesh_src(key, part):
    key = jax.random.fold_in(key, 14)
    kind_key, own_key, near_key, block_key, far_key = jax.random.split(key, 5)
    shape = (N_LAT, N_LON, EDGE)
    lat_index = jnp.arange(N_LAT, dtype=jnp.int32)[:, None, None]
    kind = jax.random.randint(kind_key, shape, 0, 20)
    own_node = 4 * MESH + jax.random.randint(own_key, shape, 0, MESH)
    block = neighbour_block(block_key, lat_index, shape)
    near_node = block * MESH + jax.random.randint(near_key, shape, 0, BORDER)
    far_node = 9 * MESH + jax.random.randint(far_key, shape, 0, N_LAT * N_LON * COARSE)
    return jnp.where(kind < 14, own_node, jnp.where(kind < 17, near_node, far_node)).astype(jnp.int32)


def draw_mesh_dst(key, part):
    key = jax.random.fold_in(key, 15)
    return jax.random.randint(key, (N_LAT, N_LON, EDGE), 0, MESH).astype(jnp.int32)


def draw_m2g_src(key, part):
    key = jax.random.fold_in(key, 16)
    kind_key, own_key, near_key, block_key = jax.random.split(key, 4)
    shape = (3, N_LAT * ROWS, N_LON * COLS)
    lat_index = (jnp.arange(N_LAT * ROWS, dtype=jnp.int32) // ROWS)[None, :, None]
    kind = jax.random.randint(kind_key, shape, 0, 4)
    own_node = 4 * MESH + jax.random.randint(own_key, shape, 0, MESH)
    block = neighbour_block(block_key, lat_index, shape)
    near_node = block * MESH + jax.random.randint(near_key, shape, 0, BORDER)
    return jnp.where(kind < 3, own_node, near_node).astype(jnp.int32)


def block_scale(stream_key, shape, shards, least, top_value):
    def one(axis_at, shards_of):
        steps = jax.random.uniform(jax.random.fold_in(jax.random.fold_in(stream_key, 6), axis_at), (shards_of,), jnp.float32, least / len(shards), top_value / len(shards))
        return jnp.repeat(jnp.exp(steps), shape[axis_at] // shards_of).reshape((-1,) + (1,) * (len(shape) - axis_at - 1))

    level = one(*shards[0])
    for cut in shards[1:]:
        level = level * one(*cut)
    return level


def gaussian(rng, extent, scale, reach, cuts=(), held_as=jnp.bfloat16):
    level = block_scale(rng, extent, cuts, -0.22, 0.18) if cuts else 1.0
    values = jax.random.normal(rng, extent, jnp.float32) * scale * level
    return jnp.minimum(jnp.maximum(values, -reach), reach).astype(held_as)


def setup_inputs(seed: int = 0) -> dict:
    splits = jax.random.split(jax.random.key(seed), 13)
    grid_latent = gaussian(splits[0], (NROWS, NCOLS, L), 1.0, 6.0, ((0, 8), (1, 16)))
    mesh_latent = gaussian(splits[1], (N_LAT, N_LON, MESH, L), 1.0, 6.0, ((0, 8), (1, 16)))
    edge_latent = gaussian(splits[2], (N_LAT, N_LON, EDGE, L), 1.0, 6.0, ((0, 8), (1, 16)))
    g2m_src = draw_g2m_src(jax.random.fold_in(splits[12], 71), 0)
    g2m_dst = draw_g2m_dst(jax.random.fold_in(splits[12], 71), 0)
    g2m_count = draw_g2m_count(jax.random.fold_in(splits[12], 71), 0)
    mesh_src = draw_mesh_src(jax.random.fold_in(splits[12], 71), 0)
    mesh_dst = draw_mesh_dst(jax.random.fold_in(splits[12], 71), 0)
    m2g_src = draw_m2g_src(jax.random.fold_in(splits[12], 71), 0)
    weights_in = gaussian(splits[9], (8 + 5 * ROUNDS, L, L), L ** -0.5, 0.25)
    weights_out = gaussian(splits[10], (4 + 2 * ROUNDS, L, L), L ** -0.5, 0.25)
    gains = jnp.clip(1.0 + 0.15 * jax.random.normal(splits[11], (4 + 2 * ROUNDS, L), jnp.float32), 0.25, 1.75)
    return dict(grid_latent=grid_latent, mesh_latent=mesh_latent, edge_latent=edge_latent, g2m_src=g2m_src, g2m_dst=g2m_dst, g2m_count=g2m_count, mesh_src=mesh_src, mesh_dst=mesh_dst, m2g_src=m2g_src, weights_in=weights_in, weights_out=weights_out, gains=gains)


epsilon = 1e-05

def finish(before, w_out, gain):
    hidden = jax.nn.silu(before).astype(jnp.bfloat16)
    result = jnp.dot(hidden, w_out, preferred_element_type=jnp.float32)
    centre = lax.optimization_barrier(jnp.mean(result, axis=-1, keepdims=True))
    centred = result - centre
    spread = lax.optimization_barrier(jnp.mean(centred * centred, axis=-1, keepdims=True))
    return centred * lax.rsqrt(spread + epsilon) * gain

def project(rows_in, weight):
    return jnp.dot(rows_in, weight, preferred_element_type=jnp.float32)

def update_node(node_rows, totals, w_self, w_total, w_out, gain):
    before = project(node_rows, w_self) + project(totals, w_total)
    return (node_rows.astype(jnp.float32) + finish(before, w_out, gain)).astype(jnp.bfloat16)

def reference(grid_latent, mesh_latent, edge_latent, g2m_src, g2m_dst, g2m_count, mesh_src, mesh_dst, m2g_src, weights_in, weights_out, gains):
    devices = jnp.arange(N_LAT * N_LON, dtype=jnp.int32)
    zero_index = jnp.zeros((), jnp.int32)
    grid_wide = jnp.pad(grid_latent, ((HALO, HALO), (HALO, HALO), (0, 0)), mode='wrap')

    def encode_one(device):
        lat_index = device // N_LON
        lon_index = device % N_LON
        grid_tile = lax.dynamic_slice(grid_wide, (lat_index * ROWS, lon_index * COLS, zero_index), (ROWS + 2 * HALO, COLS + 2 * HALO, L)).reshape(-1, L)
        mesh_own = mesh_latent[lat_index, lon_index]
        senders = g2m_src[lat_index, lon_index]
        targets = g2m_dst[lat_index, lon_index]
        grid_proj = project(grid_tile, weights_in[0])
        mesh_proj = project(mesh_own, weights_in[1])
        message = finish(grid_proj[senders] + mesh_proj[targets], weights_out[0], gains[0]).astype(jnp.bfloat16)
        alive = jnp.arange(G2M, dtype=jnp.int32) < g2m_count[lat_index, lon_index]
        message = jnp.where(alive[:, None], message, jnp.zeros_like(message))
        totals = jax.ops.segment_sum(message.astype(jnp.float32), targets, num_segments=MESH)
        return update_node(mesh_own, totals.astype(jnp.bfloat16), weights_in[2], weights_in[3], weights_out[1], gains[1])
    mesh_rows = lax.map(encode_one, devices).reshape(N_LAT, N_LON, MESH, L)
    edge_rows = edge_latent
    for layer_index in range(ROUNDS):
        first_slot = 4 + 5 * layer_index
        mesh_wide = jnp.pad(mesh_rows, ((1, 1), (1, 1), (0, 0), (0, 0)), mode='wrap')
        coarse_all = mesh_rows[:, :, MESH - COARSE:, :].reshape(-1, L)

        def process_one(device, mesh_wide=mesh_wide, coarse_all=coarse_all, mesh_rows=mesh_rows, edge_rows=edge_rows, first_slot=first_slot, layer_index=layer_index):
            lat_index = device // N_LON
            lon_index = device % N_LON
            nearby = lax.dynamic_slice(mesh_wide, (lat_index, lon_index, zero_index, zero_index), (3, 3, MESH, L)).reshape(-1, L)
            table = jnp.concatenate([nearby, coarse_all], axis=0)
            mesh_own = mesh_rows[lat_index, lon_index]
            edges_own = edge_rows[lat_index, lon_index]
            senders = mesh_src[lat_index, lon_index]
            targets = mesh_dst[lat_index, lon_index]
            sender_proj = project(table, weights_in[first_slot + 1])
            before = project(edges_own, weights_in[first_slot]) + sender_proj[senders] + project(mesh_own, weights_in[first_slot + 2])[targets]
            edges_new = (edges_own.astype(jnp.float32) + finish(before, weights_out[2 + 2 * layer_index], gains[2 + 2 * layer_index])).astype(jnp.bfloat16)
            totals = jax.ops.segment_sum(edges_new.astype(jnp.float32), targets, num_segments=MESH)
            mesh_new = update_node(mesh_own, totals.astype(jnp.bfloat16), weights_in[first_slot + 3], weights_in[first_slot + 4], weights_out[3 + 2 * layer_index], gains[3 + 2 * layer_index])
            return (mesh_new, edges_new)
        mesh_new, edges_new = lax.map(process_one, devices)
        mesh_rows = mesh_new.reshape(N_LAT, N_LON, MESH, L)
        edge_rows = edges_new.reshape(N_LAT, N_LON, EDGE, L)
    mesh_wide = jnp.pad(mesh_rows, ((1, 1), (1, 1), (0, 0), (0, 0)), mode='wrap')
    last_in = 4 + 5 * ROUNDS
    last_out = 2 + 2 * ROUNDS

    def decode_one(device):
        lat_index = device // N_LON
        lon_index = device % N_LON
        nearby = lax.dynamic_slice(mesh_wide, (lat_index, lon_index, zero_index, zero_index), (3, 3, MESH, L)).reshape(-1, L)
        grid_own = lax.dynamic_slice(grid_latent, (lat_index * ROWS, lon_index * COLS, zero_index), (ROWS, COLS, L)).reshape(-1, L)
        corners = lax.dynamic_slice(m2g_src, (zero_index, lat_index * ROWS, lon_index * COLS), (3, ROWS, COLS)).reshape(3, -1)
        sender_proj = project(nearby, weights_in[last_in])
        own_proj = project(grid_own, weights_in[last_in + 1])
        totals = jnp.zeros((ROWS * COLS, L), jnp.float32)
        for corner in range(3):
            totals = totals + finish(sender_proj[corners[corner]] + own_proj, weights_out[last_out], gains[last_out])
        return update_node(grid_own, totals.astype(jnp.bfloat16), weights_in[last_in + 2], weights_in[last_in + 3], weights_out[last_out + 1], gains[last_out + 1])
    result = lax.map(decode_one, devices).reshape(N_LAT, N_LON, ROWS, COLS, L)
    return result.transpose(0, 2, 1, 3, 4).reshape(N_LAT * ROWS, N_LON * COLS, L)
```

```python
import jax
import jax.numpy as jnp
from jax import lax
from jax.experimental import pallas as pl
from jax.experimental.pallas import tpu as pltpu
from jax.sharding import PartitionSpec as P

L = 512
ROWS = 8
COLS = 128
MESH = 320
BORDER = 64
COARSE = 16
EDGE = 2560
G2M = 1536
ROUNDS = 2
CELLS = ROWS * COLS
N_LAT = 8
N_LON = 16
OUT = 18

NORTH, SOUTH, STRIPS = 1024, 1280, 1536
GRID_ROWS = 1632
NEAR_AT, COARSE_AT, WIDE = 640, 1152, 3200
DEC_OWN, DEC_WIDE = 384, 896

TILE = 256
EPSILON = 1e-05
F32 = jnp.float32
BF16 = jnp.bfloat16
NEIGHBOURS = [(p, q) for p in (-1, 0, 1) for q in (-1, 0, 1) if (p, q) != (0, 0)]
PARTS = [(pl.ds(0, 256), "xyz"), (pl.ds(256, 256), "zxy")]


def dot(a, b):
    return jnp.dot(a, b, preferred_element_type=F32)


def hidden(before):
    half = 0.5 * before
    return (half + half * jnp.tanh(half)).astype(BF16)


def norm(result, gain):
    centre = jnp.sum(result, axis=-1, keepdims=True) * (1.0 / L)
    centred = result - centre
    spread = jnp.sum(centred * centred, axis=-1, keepdims=True) * (1.0 / L)
    return centred * lax.rsqrt(spread + EPSILON) * gain


def ones_where(mask):
    return jnp.where(mask, 1.0, 0.0).astype(BF16)


def steps_below(value, size, count):
    index = jnp.zeros_like(value)
    for step in range(1, count):
        index = index + jnp.where(value >= step * size, 1, 0)
    return index


def near_slot(source, own_at, near_at):
    block = steps_below(source, MESH, 9)
    row = source - block * MESH
    slot = block - jnp.where(block > 4, 1, 0)
    return jnp.where(block == 4, own_at + row, near_at + slot * BORDER + row)


def grid_slot(cell):
    r = steps_below(cell, COLS + 4, ROWS + 4)
    c = cell - r * (COLS + 4)
    north, south = r < 2, r >= ROWS + 2
    west, east = c < 2, c >= COLS + 2
    row = jnp.where(north, NORTH // COLS + r, jnp.where(south, SOUTH // COLS + r - (ROWS + 2), r - 2))
    inside = row * COLS + c - 2
    strip = jnp.where(north, 2, jnp.where(south, 4, 0)) + jnp.where(east, 1, 0)
    strip_row = jnp.where(north, r + ROWS - 2, jnp.where(south, r - (ROWS + 2), r - 2))
    strip_col = jnp.where(east, c - (COLS + 2), c)
    side = STRIPS + strip * 16 + strip_row * 2 + strip_col
    return jnp.where(west | east, side, inside)


def kernel(
    grid, mesh_in, edge_in, g2m_src, g2m_dst, g2m_count, mesh_src, mesh_dst, m2g_src,
    weights_in, weights_out, gains, out,
    w, cells, table, edges, acc, pick, place, coarse, near, proj, message, mesh_now, strips, square,
    local_sem, send_sem, recv_sem,
):
    lat, lon = lax.axis_index("lat"), lax.axis_index("lon")
    z, core = lax.div(lat, 2), lax.rem(lat, 2)
    x, y = lax.div(lon, 4), lax.rem(lon, 4)
    counts = {"local": 0, "remote": 0}

    def local(src, dst):
        i = counts["local"]
        counts["local"] += 1
        copy = pltpu.make_async_copy(src, dst, local_sem.at[i])
        copy.start()
        return copy

    def remote(src, dst, device):
        i = counts["remote"]
        counts["remote"] += 1
        copy = pltpu.make_async_remote_copy(
            src_ref=src, dst_ref=dst, send_sem=send_sem.at[i], recv_sem=recv_sem.at[i],
            device_id=device, device_id_type=pl.DeviceIdType.MESH,
        )
        copy.start()
        return copy

    def beside(p, q):
        return (lax.rem(lat + (p + N_LAT), N_LAT), lax.rem(lon + (q + N_LON), N_LON))

    def along(axis, d):
        if axis == "x":
            return (lat, lax.rem(x + d, 4) * 4 + y)
        if axis == "y":
            return (lat, x * 4 + lax.rem(y + d, 4))
        return (lax.rem(z + d, 4) * 2 + core, lon)

    sibling = (z * 2 + (1 - core), lon)

    got_grid = local(grid, cells.at[pl.ds(0, CELLS)])
    got_weights = []
    for first, many, first_out, many_out in ((0, 4, 0, 2), (4, 5, 2, 2), (9, 5, 4, 2), (14, 4, 6, 2)):
        got_weights.append((
            local(weights_in.at[pl.ds(first, many)], w.at[pl.ds(first, many)]),
            local(weights_out.at[pl.ds(first_out, many_out)], w.at[pl.ds(OUT + first_out, many_out)]),
        ))
        if first == 0:
            got_edges = local(edge_in, edges)

    barrier = pltpu.get_barrier_semaphore()
    peers = [beside(p, q) for p, q in NEIGHBOURS]
    peers += [along(axis, d) for axis in "xyz" for d in (1, 2, 3)] + [sibling]
    for peer in peers:
        pl.semaphore_signal(barrier, inc=1, device_id=peer, device_id_type=pl.DeviceIdType.MESH)
    pl.semaphore_wait(barrier, len(peers))

    halo = [
        remote(grid.at[pl.ds(CELLS - 256, 256)], cells.at[pl.ds(NORTH, 256)], beside(1, 0)),
        remote(grid.at[pl.ds(0, 256)], cells.at[pl.ds(SOUTH, 256)], beside(-1, 0)),
    ]
    got_grid.wait()
    i = lax.broadcasted_iota(jnp.int32, (16, COLS), 0)
    j = lax.broadcasted_iota(jnp.int32, (16, COLS), 1)
    for side, first, shift in ((0, COLS - 16, 14), (1, 0, 0)):
        rim = jnp.concatenate([cells[r * COLS + first : r * COLS + first + 16] for r in range(ROWS)], axis=0)
        wanted = (i >> 1) * 16 + shift + (i & 1)
        strips[side] = dot(ones_where(j == wanted), rim).astype(BF16)
    for side, q in ((0, 1), (1, -1)):
        for place_at, p in ((0, 0), (2, 1), (4, -1)):
            halo.append(remote(
                strips.at[side], cells.at[pl.ds(STRIPS + (place_at + side) * 16, 16)], beside(p, q)
            ))

    lanes = lax.broadcasted_iota(jnp.int32, (128, 128), 1).astype(F32)
    nodes = lax.broadcasted_iota(jnp.int32, (MESH, 128), 0)

    def columns(index, at):
        many = index.shape[0]
        square[...] = jnp.zeros_like(square)
        square[0:many] = index.astype(F32)
        turned = square[...].T
        for t in range(many):
            acc[t * 128 : t * 128 + 128, at : at + 128] = jnp.broadcast_to(turned[:, t : t + 1], (128, 128))

    live = g2m_count[...]
    lane = lax.broadcasted_iota(jnp.int32, (1, 128), 1)
    for t in range(G2M // 128):
        target = jnp.where(lane + t * 128 < live, g2m_dst[t : t + 1, :], -1)
        place[:, EDGE + t * 128 : EDGE + t * 128 + 128] = ones_where(nodes == target)
    for t in range(EDGE // 128):
        place[:, t * 128 : t * 128 + 128] = ones_where(nodes == mesh_dst[t : t + 1, :])

    columns(grid_slot(g2m_src[...]), 0)
    columns(g2m_dst[...] + GRID_ROWS, 128)

    @pl.loop(0, G2M // 128)
    def _(t):
        rows = pl.ds(pl.multiple_of(t * 128, 128), 128)
        first, second = acc[rows, 0:128], acc[rows, 128:256]
        for chunk in range(16):
            ids = lanes + float(chunk * 128)
            if chunk < 12:
                mask = first == ids
            elif chunk == 12:
                mask = (first == ids) | (second == ids)
            else:
                mask = second == ids
            pick[rows, chunk * 128 : chunk * 128 + 128] = ones_where(mask)

    got_weights[0][0].wait()
    got_weights[0][1].wait()

    @pl.loop(0, CELLS // TILE)
    def _(t):
        rows = pl.ds(pl.multiple_of(t * TILE, TILE), TILE)
        table[rows, :] = dot(cells[rows, :], w[0]).astype(BF16)

    table[GRID_ROWS : GRID_ROWS + MESH] = dot(mesh_in[...], w[1]).astype(BF16)
    table[GRID_ROWS + MESH :] = jnp.zeros((2048 - GRID_ROWS - MESH, L), BF16)
    for copy in halo:
        copy.wait_recv()
    table[CELLS:GRID_ROWS] = dot(cells[CELLS:GRID_ROWS], w[0]).astype(BF16)

    @pl.loop(0, G2M // TILE)
    def _(t):
        rows = pl.ds(pl.multiple_of(t * TILE, TILE), TILE)
        before = dot(pick[rows, 0:2048], table[...])
        message[rows, :] = norm(dot(hidden(before), w[OUT]), gains[0:1, :]).astype(BF16)

    def new_nodes(old, totals, first, k):
        before = dot(old, w[first]) + dot(totals.astype(BF16), w[first + 1])
        return (old.astype(F32) + norm(dot(hidden(before), w[OUT + k]), gains[k : k + 1, :])).astype(BF16)

    totals = dot(place[:, EDGE : EDGE + G2M], message[...])
    mesh_now[...] = new_nodes(mesh_in[...], totals, 2, 1)

    sent = list(halo)

    def send_near(r):
        copies = []
        for slot, (p, q) in enumerate(NEIGHBOURS):
            copies.append(remote(proj.at[r, pl.ds(0, BORDER)], near.at[r, slot], beside(-p, -q)))
        sent.extend(copies)
        return copies

    def block(r, part, known):
        at = {"x": x, "y": y, "z": z}
        for axis in known:
            at[axis] = slice(None)
        return coarse.at[r, at["z"], core, at["x"], at["y"], :, part]

    def stage(r, part, order, step):
        known = order[:step]
        ref = block(r, part, known)
        copies = [remote(ref, ref, along(order[step], d)) for d in (1, 2, 3)]
        sent.extend(copies)
        return copies

    def arrived(r, part, order, d):
        at = {"x": x, "y": y, "z": z}
        at[order[2]] = lax.rem(at[order[2]] + (4 - d), 4)
        for axis in order[:2]:
            at[axis] = slice(None)
        return coarse.at[r, at["z"], core, at["x"], at["y"], :, part]

    for r in range(ROUNDS):
        first = 4 + 5 * r
        got_weights[1 + r][0].wait()
        got_weights[1 + r][1].wait()
        sender = dot(mesh_now[...], w[first + 1]).astype(BF16)
        proj[r, 0:MESH] = sender
        coarse[r, z, core, x, y] = sender[MESH - COARSE :]
        moving = [stage(r, part, order, 0) for part, order in PARTS]
        got_near = send_near(r)
        proj[r, MESH : 2 * MESH] = dot(mesh_now[...], w[first + 2]).astype(BF16)

        def wait_stage(step):
            for k, (part, order) in enumerate(PARTS):
                for copy in moving[k]:
                    copy.wait_recv()
                moving[k] = stage(r, part, order, step)

        if r == 0:
            got_edges.wait()
            source = mesh_src[...]
            slot = jnp.where(source >= 9 * MESH, COARSE_AT - 9 * MESH + source, near_slot(source, 0, NEAR_AT))
            columns(slot, 0)
            columns(mesh_dst[...] + MESH, 128)

            @pl.loop(0, EDGE // 128)
            def _(t):
                rows = pl.ds(pl.multiple_of(t * 128, 128), 128)
                one, two = acc[rows, 0:128], acc[rows, 128:256]
                for chunk in range(WIDE // 128):
                    ids = lanes + float(chunk * 128)
                    if chunk in (3, 4):
                        mask = two == ids
                    elif chunk == 2:
                        mask = (one == ids) | (two == ids)
                    else:
                        mask = one == ids
                    pick[rows, chunk * 128 : chunk * 128 + 128] = ones_where(mask)

        wait_stage(1)

        def own_part(t):
            rows = pl.ds(pl.multiple_of(t * TILE, TILE), TILE)
            acc[rows, :] = dot(edges[rows, :], w[first]) + dot(pick[rows, 0:NEAR_AT], proj[r])

        pl.loop(0, 5)(own_part)
        wait_stage(2)
        across = []
        for part, order in PARTS:
            ref = block(r, part, order[:2])
            across.append(remote(ref, ref, sibling))
        pl.loop(5, 10)(own_part)
        for copy in got_near:
            copy.wait_recv()

        @pl.loop(0, EDGE // TILE)
        def _(t):
            rows = pl.ds(pl.multiple_of(t * TILE, TILE), TILE)
            acc[rows, :] += dot(pick[rows, NEAR_AT:COARSE_AT], near[r].reshape(8 * BORDER, L))

        for d in (1, 2, 3):
            for k, (part, order) in enumerate(PARTS):
                moving[k][d - 1].wait_recv()
                ref = arrived(r, part, order, d)
                across.append(remote(ref, ref, sibling))
        sent.extend(across)
        for copy in across:
            copy.wait_recv()

        @pl.loop(0, EDGE // TILE)
        def _(t):
            rows = pl.ds(pl.multiple_of(t * TILE, TILE), TILE)
            before = acc[rows, :] + dot(pick[rows, COARSE_AT:WIDE], coarse[r].reshape(2048, L))
            update = norm(dot(hidden(before), w[OUT + 2 + 2 * r]), gains[2 + 2 * r : 3 + 2 * r, :])
            edges[rows, :] = (edges[rows, :].astype(F32) + update).astype(BF16)

        totals = dot(place[:, 0:EDGE], edges[...])
        mesh_now[...] = new_nodes(mesh_now[...], totals, first + 3, 3 + 2 * r)

    got_weights[3][0].wait()
    got_weights[3][1].wait()
    proj[ROUNDS, 0:MESH] = dot(mesh_now[...], w[14]).astype(BF16)
    got_near = send_near(ROUNDS)
    proj[ROUNDS, MESH : 2 * MESH] = jnp.zeros((MESH, L), BF16)

    columns(near_slot(m2g_src[...], 0, DEC_OWN), 0)

    @pl.loop(0, ROWS)
    def _(t):
        to = pl.ds(pl.multiple_of(t * 128, 128), 128)
        for corner in range(3):
            one = acc[pl.ds(pl.multiple_of(corner * CELLS + t * 128, 128), 128), 0:128]
            for chunk in range(DEC_WIDE // 128):
                at = corner * DEC_WIDE + chunk * 128
                pick[to, at : at + 128] = ones_where(one == lanes + float(chunk * 128))

    @pl.loop(0, CELLS // TILE)
    def _(t):
        rows = pl.ds(pl.multiple_of(t * TILE, TILE), TILE)
        base = dot(cells[rows, :], w[15])
        for corner in range(3):
            at = corner * DEC_WIDE
            to = pl.ds(pl.multiple_of(corner * CELLS + t * TILE, TILE), TILE)
            acc[to, :] = base + dot(pick[rows, at : at + DEC_OWN], proj[ROUNDS, 0:DEC_OWN])

    for copy in got_near:
        copy.wait_recv()

    @pl.loop(0, CELLS // TILE)
    def _(t):
        rows = pl.ds(pl.multiple_of(t * TILE, TILE), TILE)
        totals = jnp.zeros((TILE, L), F32)
        for corner in range(3):
            at = corner * DEC_WIDE
            to = pl.ds(pl.multiple_of(corner * CELLS + t * TILE, TILE), TILE)
            before = acc[to, :] + dot(
                pick[rows, at + DEC_OWN : at + DEC_WIDE], near[ROUNDS].reshape(8 * BORDER, L)
            )
            totals = totals + norm(dot(hidden(before), w[OUT + 6]), gains[6:7, :])
        out[rows, :] = new_nodes(cells[rows, :], totals, 16, 7)

    for copy in sent:
        copy.wait_send()


def on_device(
    grid_latent, mesh_latent, edge_latent, g2m_src, g2m_dst, g2m_count, mesh_src, mesh_dst, m2g_src,
    weights_in, weights_out, gains,
):
    anywhere = pl.BlockSpec(memory_space=pl.ANY)
    vmem = pl.BlockSpec(memory_space=pltpu.VMEM)
    result = pl.pallas_call(
        kernel,
        out_shape=jax.ShapeDtypeStruct((CELLS, L), BF16),
        in_specs=[anywhere, vmem, anywhere] + [vmem] * 6 + [anywhere, anywhere, vmem],
        out_specs=vmem,
        scratch_shapes=[
            pltpu.VMEM((26, L, L), BF16),
            pltpu.VMEM((GRID_ROWS, L), BF16),
            pltpu.VMEM((2048, L), BF16),
            pltpu.VMEM((EDGE, L), BF16),
            pltpu.VMEM((3 * CELLS, L), F32),
            pltpu.VMEM((EDGE, WIDE), BF16),
            pltpu.VMEM((MESH, EDGE + G2M), BF16),
            pltpu.VMEM((ROUNDS, 4, 2, 4, 4, COARSE, L), BF16),
            pltpu.VMEM((ROUNDS + 1, 8, BORDER, L), BF16),
            pltpu.VMEM((ROUNDS + 1, 2 * MESH, L), BF16),
            pltpu.VMEM((G2M, L), BF16),
            pltpu.VMEM((MESH, L), BF16),
            pltpu.VMEM((2, 16, L), BF16),
            pltpu.VMEM((128, 128), F32),
            pltpu.SemaphoreType.DMA((10,)),
            pltpu.SemaphoreType.DMA((84,)),
            pltpu.SemaphoreType.DMA((84,)),
        ],
        compiler_params=pltpu.CompilerParams(
            collective_id=0, has_side_effects=True, vmem_limit_bytes=62 * 1024 * 1024
        ),
        cost_estimate=pl.CostEstimate(flops=40_000_000_000, bytes_accessed=20_000_000, transcendentals=10_000_000),
    )(
        grid_latent.reshape(CELLS, L), mesh_latent.reshape(MESH, L), edge_latent.reshape(EDGE, L),
        g2m_src.reshape(-1, 128), g2m_dst.reshape(-1, 128), g2m_count,
        mesh_src.reshape(-1, 128), mesh_dst.reshape(-1, 128), m2g_src.reshape(-1, 128),
        weights_in, weights_out, gains,
    )
    return result.reshape(grid_latent.shape)


def solution(mesh):
    placed = (
        P("lat", "lon", None),
        P("lat", "lon", None, None),
        P("lat", "lon", None, None),
        P("lat", "lon", None),
        P("lat", "lon", None),
        P("lat", "lon"),
        P("lat", "lon", None),
        P("lat", "lon", None),
        P(None, "lat", "lon"),
        P(),
        P(),
        P(),
    )
    return jax.shard_map(
        on_device, mesh=mesh, in_specs=placed, out_specs=P("lat", "lon", None), check_vma=False
    )
```

```python
import jax
import jax.numpy as jnp
from jax import lax
from jax.experimental import pallas as pl
from jax.experimental.pallas import tpu as pltpu
from jax.sharding import PartitionSpec as P

L = 512
ROWS = 8
COLS = 128
MESH = 320
BORDER = 64
COARSE = 16
EDGE = 2560
G2M = 1536
ROUNDS = 2
CELLS = ROWS * COLS
N_LAT = 8
N_LON = 16
OUT = 18

NORTH, SOUTH, STRIPS = 1408, 1664, 1920
GRID_ROWS = 1632
NEAR_AT, COARSE_AT, WIDE = 640, 1152, 3200
DEC_OWN, DEC_WIDE = 384, 896

TILE = 512
EPSILON = 1e-05
F32 = jnp.float32
BF16 = jnp.bfloat16
NEIGHBOURS = [(p, q) for p in (-1, 0, 1) for q in (-1, 0, 1) if (p, q) != (0, 0)]
XY = [(i, j, 0) for i in range(4) for j in range(4) if (i, j) != (0, 0)]
YZ = [(0, i, j) for i in range(4) for j in range(4) if (i, j) != (0, 0)]
PARTS = [(pl.ds(0, 256), "z", XY), (pl.ds(256, 256), "x", YZ)]


def dot(a, b):
    return jnp.dot(a, b, preferred_element_type=F32)


def hidden(before):
    half = 0.5 * before
    return (half + half * jnp.tanh(half)).astype(BF16)


def norm(result, gain):
    centre = jnp.sum(result, axis=-1, keepdims=True) * (1.0 / L)
    centred = result - centre
    spread = jnp.sum(centred * centred, axis=-1, keepdims=True) * (1.0 / L)
    return centred * lax.rsqrt(spread + EPSILON) * gain


def ones_where(mask):
    return jnp.where(mask, 1.0, 0.0).astype(BF16)


def steps_below(value, size, count):
    index = jnp.zeros_like(value)
    for step in range(1, count):
        index = index + jnp.where(value >= step * size, 1, 0)
    return index


def near_slot(source, own_at, near_at):
    block = steps_below(source, MESH, 9)
    row = source - block * MESH
    slot = block - jnp.where(block > 4, 1, 0)
    return jnp.where(block == 4, own_at + row, near_at + slot * BORDER + row)


def grid_slot(cell):
    r = steps_below(cell, COLS + 4, ROWS + 4)
    c = cell - r * (COLS + 4)
    north, south = r < 2, r >= ROWS + 2
    west, east = c < 2, c >= COLS + 2
    inside = (r - 2) * COLS + c - 2
    inside = jnp.where(north, NORTH + r * COLS + c - 2, inside)
    inside = jnp.where(south, SOUTH + (r - (ROWS + 2)) * COLS + c - 2, inside)
    strip = jnp.where(north, 2, jnp.where(south, 4, 0)) + jnp.where(east, 1, 0)
    strip_row = jnp.where(north, r + ROWS - 2, jnp.where(south, r - (ROWS + 2), r - 2))
    strip_col = jnp.where(east, c - (COLS + 2), c)
    side = STRIPS + strip * 16 + strip_row * 2 + strip_col
    return jnp.where(west | east, side, inside)


def edge_slot(source, core):
    far = source - 9 * MESH
    other = ((far >> 8) + core) & 1
    coarse = COARSE_AT + other * 1024 + (far >> 9) * 256 + (far & 255)
    return jnp.where(far >= 0, coarse, near_slot(source, 0, NEAR_AT))


def kernel(
    grid, mesh_in, edge_in, g2m_src, g2m_dst, g2m_count, mesh_src, mesh_dst, m2g_src,
    weights_in, weights_out, gains, out,
    w, cells, table, edges, acc, pick, place, coarse, near, proj, message, mesh_now, own_part, strips, square,
    local_sem, send_sem, recv_sem,
):
    lat, lon = lax.axis_index("lat"), lax.axis_index("lon")
    z, core = lax.div(lat, 2), lax.rem(lat, 2)
    x, y = lax.div(lon, 4), lax.rem(lon, 4)
    counts = {"local": 0, "remote": 0}

    def local(src, dst):
        i = counts["local"]
        counts["local"] += 1
        copy = pltpu.make_async_copy(src, dst, local_sem.at[i])
        copy.start()
        return copy

    def remote(src, dst, device):
        i = counts["remote"]
        counts["remote"] += 1
        copy = pltpu.make_async_remote_copy(
            src_ref=src, dst_ref=dst, send_sem=send_sem.at[i], recv_sem=recv_sem.at[i],
            device_id=device, device_id_type=pl.DeviceIdType.MESH,
        )
        copy.start()
        return copy

    def beside(p, q):
        return (lax.rem(lat + (p + N_LAT), N_LAT), lax.rem(lon + (q + N_LON), N_LON))

    def chip(dx, dy, dz):
        return (lax.rem(z + dz, 4) * 2 + core, lax.rem(x + dx, 4) * 4 + lax.rem(y + dy, 4))

    sibling = (z * 2 + (1 - core), lon)

    got_grid = local(grid, cells.at[pl.ds(0, CELLS)])
    got_weights = []
    for first, many, first_out, many_out in ((0, 4, 0, 2), (4, 5, 2, 2), (9, 5, 4, 2), (14, 4, 6, 2)):
        got_weights.append((
            local(weights_in.at[pl.ds(first, many)], w.at[pl.ds(first, many)]),
            local(weights_out.at[pl.ds(first_out, many_out)], w.at[pl.ds(OUT + first_out, many_out)]),
        ))
        if first == 0:
            got_edges = local(edge_in, edges)

    barrier = pltpu.get_barrier_semaphore()
    peers = [beside(p, q) for p, q in NEIGHBOURS] + [chip(*d) for d in sorted(set(XY + YZ))] + [sibling]
    for peer in peers:
        pl.semaphore_signal(barrier, inc=1, device_id=peer, device_id_type=pl.DeviceIdType.MESH)

    got_grid.wait()
    i = lax.broadcasted_iota(jnp.int32, (16, COLS), 0)
    j = lax.broadcasted_iota(jnp.int32, (16, COLS), 1)
    for side, first, shift in ((0, COLS - 16, 14), (1, 0, 0)):
        rim = jnp.concatenate([cells[r * COLS + first : r * COLS + first + 16] for r in range(ROWS)], axis=0)
        wanted = (i >> 1) * 16 + shift + (i & 1)
        strips[side] = dot(ones_where(j == wanted), rim).astype(BF16)

    pl.semaphore_wait(barrier, len(peers))
    halo = [
        remote(grid.at[pl.ds(CELLS - 256, 256)], cells.at[pl.ds(CELLS, 256)], beside(1, 0)),
        remote(grid.at[pl.ds(0, 256)], cells.at[pl.ds(CELLS + 256, 256)], beside(-1, 0)),
    ]
    for side, q in ((0, 1), (1, -1)):
        for place_at, p in ((0, 0), (2, 1), (4, -1)):
            to = CELLS + 512 + (place_at + side) * 16
            halo.append(remote(strips.at[side], cells.at[pl.ds(to, 16)], beside(p, q)))

    lanes = lax.broadcasted_iota(jnp.int32, (128, 128), 1).astype(F32)
    nodes = lax.broadcasted_iota(jnp.int32, (MESH, 128), 0)

    def stacked(ref):
        square[...] = jnp.zeros_like(square)
        many = ref.shape[1] // 128
        for t in range(many):
            square[t : t + 1, :] = ref[0:1, t * 128 : t * 128 + 128].astype(F32)
        return square[...].astype(jnp.int32), many

    def columns(index, many, at):
        turned = index.astype(F32).T
        for t in range(many):
            acc[t * 128 : t * 128 + 128, at : at + 128] = jnp.broadcast_to(turned[:, t : t + 1], (128, 128))

    source, many = stacked(g2m_src)
    columns(grid_slot(source), many, 0)
    target, many = stacked(g2m_dst)
    columns(target + CELLS, many, 128)

    @pl.loop(0, G2M // 128)
    def _(t):
        rows = pl.ds(pl.multiple_of(t * 128, 128), 128)
        first, second = acc[rows, 0:128], acc[rows, 128:256]
        for chunk in range(16):
            ids = lanes + float(chunk * 128)
            mask = (second if 8 <= chunk < 11 else first) == ids
            pick[rows, chunk * 128 : chunk * 128 + 128] = ones_where(mask)

    live = g2m_count[...]
    lane = lax.broadcasted_iota(jnp.int32, (1, 128), 1)
    for t in range(G2M // 128):
        target = jnp.where(lane + t * 128 < live, g2m_dst[0:1, t * 128 : t * 128 + 128], -1)
        place[:, EDGE + t * 128 : EDGE + t * 128 + 128] = ones_where(nodes == target)

    got_weights[0][0].wait()
    got_weights[0][1].wait()

    @pl.loop(0, CELLS // TILE)
    def _(t):
        rows = pl.ds(pl.multiple_of(t * TILE, TILE), TILE)
        table[rows, :] = dot(cells[rows, :], w[0]).astype(BF16)

    table[CELLS : CELLS + MESH] = dot(mesh_in[...], w[1]).astype(BF16)
    table[CELLS + MESH : NORTH] = jnp.zeros((NORTH - CELLS - MESH, L), BF16)
    table[NORTH + 608 :] = jnp.zeros((2048 - NORTH - 608, L), BF16)
    own_part[...] = dot(mesh_in[...], w[2])

    @pl.loop(0, G2M // TILE)
    def _(t):
        rows = pl.ds(pl.multiple_of(t * TILE, TILE), TILE)
        acc[rows, :] = dot(pick[rows, 0:NORTH], table[0:NORTH])

    for copy in halo:
        copy.wait_recv()
    table[NORTH : NORTH + 608] = dot(cells[CELLS:GRID_ROWS], w[0]).astype(BF16)

    @pl.loop(0, G2M // TILE)
    def _(t):
        rows = pl.ds(pl.multiple_of(t * TILE, TILE), TILE)
        before = acc[rows, :] + dot(pick[rows, NORTH:2048], table[NORTH:2048])
        message[rows, :] = norm(dot(hidden(before), w[OUT]), gains[0:1, :]).astype(BF16)

    def new_nodes(old, self_part, totals, second, k):
        before = self_part + dot(totals.astype(BF16), w[second])
        return (old.astype(F32) + norm(dot(hidden(before), w[OUT + k]), gains[k : k + 1, :])).astype(BF16)

    def update_encoded(a, b):
        totals = dot(place[a:b, EDGE : EDGE + G2M], message[...])
        mesh_now[a:b] = new_nodes(mesh_in[a:b], own_part[a:b], totals, 3, 1)

    def update_round(r):
        def update(a, b):
            totals = dot(place[a:b, 0:EDGE], edges[...])
            mesh_now[a:b] = new_nodes(mesh_now[a:b], own_part[a:b], totals, 8 + 5 * r, 3 + 2 * r)

        return update

    sent = list(halo)

    def send_near(r):
        copies = []
        for slot, (p, q) in enumerate(NEIGHBOURS):
            copies.append(remote(proj.at[r, pl.ds(0, BORDER)], near.at[r, slot], beside(-p, -q)))
        sent.extend(copies)
        return copies

    def plane(r, part, axis, d):
        here = lax.rem({"x": x, "z": z}[axis] + (4 - d), 4)
        if axis == "z":
            return coarse.at[r, 0, here, :, :, :, part]
        return coarse.at[r, 0, :, here, :, :, part]

    update = update_encoded
    for r in range(ROUNDS):
        first = 4 + 5 * r
        got_weights[1 + r][0].wait()
        got_weights[1 + r][1].wait()
        update(MESH - COARSE, MESH)
        coarse[r, 0, z, x, y] = dot(mesh_now[MESH - COARSE : MESH], w[first + 1]).astype(BF16)
        arriving = []
        for part, axis, offsets in PARTS:
            ref = coarse.at[r, 0, z, x, y, :, part]
            arriving.append([remote(ref, ref, chip(*d)) for d in offsets])
            sent.extend(arriving[-1])
        update(0, MESH - COARSE)
        proj[r, 0:MESH] = dot(mesh_now[...], w[first + 1]).astype(BF16)
        got_near = send_near(r)
        proj[r, MESH : 2 * MESH] = dot(mesh_now[...], w[first + 2]).astype(BF16)
        own_part[...] = dot(mesh_now[...], w[first + 3])

        if r == 0:
            got_edges.wait()
            source, many = stacked(mesh_src)
            columns(edge_slot(source, core), many, 0)
            target, many = stacked(mesh_dst)
            columns(target + MESH, many, 128)

        across = []

        def second_stage():
            moving = []
            for k, (part, axis, offsets) in enumerate(PARTS):
                for copy in arriving[k]:
                    copy.wait_recv()
                ref = plane(r, part, axis, 0)
                moving.append([
                    remote(ref, ref, chip(**{"dx": 0, "dy": 0, "dz": 0, "d" + axis: d})) for d in (1, 2, 3)
                ])
                sent.extend(moving[-1])
            for part, axis, offsets in PARTS:
                across.append(forward(part, axis, 0))
            return moving

        def forward(part, axis, d):
            here = lax.rem({"x": x, "z": z}[axis] + (4 - d), 4)
            if axis == "z":
                return remote(
                    coarse.at[r, 0, here, :, :, :, part], coarse.at[r, 1, here, :, :, :, part], sibling
                )
            return remote(
                coarse.at[r, 0, :, here, :, :, part], coarse.at[r, 1, :, here, :, :, part], sibling
            )

        if r == 0:

            @pl.loop(0, EDGE // 128)
            def _(t):
                rows = pl.ds(pl.multiple_of(t * 128, 128), 128)
                one, two = acc[rows, 0:128], acc[rows, 128:256]
                for chunk in range(WIDE // 128):
                    ids = lanes + float(chunk * 128)
                    if chunk in (3, 4):
                        mask = two == ids
                    elif chunk == 2:
                        mask = (one == ids) | (two == ids)
                    else:
                        mask = one == ids
                    pick[rows, chunk * 128 : chunk * 128 + 128] = ones_where(mask)

            moving = second_stage()
            for t in range(EDGE // 128):
                place[:, t * 128 : t * 128 + 128] = ones_where(nodes == mesh_dst[0:1, t * 128 : t * 128 + 128])

        @pl.loop(0, EDGE // TILE)
        def _(t):
            rows = pl.ds(pl.multiple_of(t * TILE, TILE), TILE)
            acc[rows, :] = dot(edges[rows, :], w[first]) + dot(pick[rows, 0:NEAR_AT], proj[r])

        if r > 0:
            moving = second_stage()
        for copy in got_near:
            copy.wait_recv()

        @pl.loop(0, EDGE // TILE)
        def _(t):
            rows = pl.ds(pl.multiple_of(t * TILE, TILE), TILE)
            acc[rows, :] += dot(pick[rows, NEAR_AT:COARSE_AT], near[r].reshape(8 * BORDER, L))

        for d in (1, 2, 3):
            for k, (part, axis, offsets) in enumerate(PARTS):
                moving[k][d - 1].wait_recv()
                across.append(forward(part, axis, d))
        sent.extend(across)

        @pl.loop(0, EDGE // TILE)
        def _(t):
            rows = pl.ds(pl.multiple_of(t * TILE, TILE), TILE)
            acc[rows, :] += dot(pick[rows, COARSE_AT : COARSE_AT + 1024], coarse[r, 0].reshape(1024, L))

        for copy in across:
            copy.wait_recv()

        @pl.loop(0, EDGE // TILE)
        def _(t):
            rows = pl.ds(pl.multiple_of(t * TILE, TILE), TILE)
            before = acc[rows, :] + dot(pick[rows, COARSE_AT + 1024 : WIDE], coarse[r, 1].reshape(1024, L))
            result = norm(dot(hidden(before), w[OUT + 2 + 2 * r]), gains[2 + 2 * r : 3 + 2 * r, :])
            edges[rows, :] = (edges[rows, :].astype(F32) + result).astype(BF16)

        update = update_round(r)

    got_weights[3][0].wait()
    got_weights[3][1].wait()
    update(0, BORDER)
    proj[ROUNDS, 0:BORDER] = dot(mesh_now[0:BORDER], w[14]).astype(BF16)
    got_near = send_near(ROUNDS)
    update(BORDER, MESH)
    proj[ROUNDS, BORDER:MESH] = dot(mesh_now[BORDER:MESH], w[14]).astype(BF16)
    proj[ROUNDS, MESH : 2 * MESH] = jnp.zeros((MESH, L), BF16)

    square[...] = jnp.zeros_like(square)
    square[0:24] = m2g_src[...].astype(F32)
    columns(near_slot(square[...].astype(jnp.int32), 0, DEC_OWN), 24, 0)

    @pl.loop(0, ROWS)
    def _(t):
        to = pl.ds(pl.multiple_of(t * 128, 128), 128)
        for corner in range(3):
            one = acc[pl.ds(pl.multiple_of(corner * CELLS + t * 128, 128), 128), 0:128]
            for chunk in range(DEC_WIDE // 128):
                at = corner * DEC_WIDE + chunk * 128
                pick[to, at : at + 128] = ones_where(one == lanes + float(chunk * 128))

    @pl.loop(0, CELLS // TILE)
    def _(t):
        rows = pl.ds(pl.multiple_of(t * TILE, TILE), TILE)
        base = dot(cells[rows, :], w[15])
        for corner in range(3):
            at = corner * DEC_WIDE
            to = pl.ds(pl.multiple_of(corner * CELLS + t * TILE, TILE), TILE)
            acc[to, :] = base + dot(pick[rows, at : at + DEC_OWN], proj[ROUNDS, 0:DEC_OWN])

    for copy in got_near:
        copy.wait_recv()

    @pl.loop(0, CELLS // TILE)
    def _(t):
        rows = pl.ds(pl.multiple_of(t * TILE, TILE), TILE)
        totals = jnp.zeros((TILE, L), F32)
        for corner in range(3):
            at = corner * DEC_WIDE
            to = pl.ds(pl.multiple_of(corner * CELLS + t * TILE, TILE), TILE)
            before = acc[to, :] + dot(
                pick[rows, at + DEC_OWN : at + DEC_WIDE], near[ROUNDS].reshape(8 * BORDER, L)
            )
            totals = totals + norm(dot(hidden(before), w[OUT + 6]), gains[6:7, :])
        out[rows, :] = new_nodes(cells[rows, :], dot(cells[rows, :], w[16]), totals, 17, 7)

    for copy in sent:
        copy.wait_send()


def on_device(
    grid_latent, mesh_latent, edge_latent, g2m_src, g2m_dst, g2m_count, mesh_src, mesh_dst, m2g_src,
    weights_in, weights_out, gains,
):
    anywhere = pl.BlockSpec(memory_space=pl.ANY)
    vmem = pl.BlockSpec(memory_space=pltpu.VMEM)
    result = pl.pallas_call(
        kernel,
        out_shape=jax.ShapeDtypeStruct((CELLS, L), BF16),
        in_specs=[anywhere, vmem, anywhere] + [vmem] * 6 + [anywhere, anywhere, vmem],
        out_specs=vmem,
        scratch_shapes=[
            pltpu.VMEM((26, L, L), BF16),
            pltpu.VMEM((GRID_ROWS, L), BF16),
            pltpu.VMEM((2048, L), BF16),
            pltpu.VMEM((EDGE, L), BF16),
            pltpu.VMEM((3 * CELLS, L), F32),
            pltpu.VMEM((EDGE, WIDE), BF16),
            pltpu.VMEM((MESH, EDGE + G2M), BF16),
            pltpu.VMEM((ROUNDS, 2, 4, 4, 4, COARSE, L), BF16),
            pltpu.VMEM((ROUNDS + 1, 8, BORDER, L), BF16),
            pltpu.VMEM((ROUNDS + 1, 2 * MESH, L), BF16),
            pltpu.VMEM((G2M, L), BF16),
            pltpu.VMEM((MESH, L), BF16),
            pltpu.VMEM((MESH, L), F32),
            pltpu.VMEM((2, 16, L), BF16),
            pltpu.VMEM((128, 128), F32),
            pltpu.SemaphoreType.DMA((10,)),
            pltpu.SemaphoreType.DMA((120,)),
            pltpu.SemaphoreType.DMA((120,)),
        ],
        compiler_params=pltpu.CompilerParams(
            collective_id=0, has_side_effects=True, vmem_limit_bytes=62 * 1024 * 1024
        ),
        cost_estimate=pl.CostEstimate(flops=40_000_000_000, bytes_accessed=20_000_000, transcendentals=10_000_000),
    )(
        grid_latent.reshape(CELLS, L), mesh_latent.reshape(MESH, L), edge_latent.reshape(EDGE, L),
        g2m_src.reshape(1, G2M), g2m_dst.reshape(1, G2M), g2m_count,
        mesh_src.reshape(1, EDGE), mesh_dst.reshape(1, EDGE), m2g_src.reshape(-1, 128),
        weights_in, weights_out, gains,
    )
    return result.reshape(grid_latent.shape)


def solution(mesh):
    placed = (
        P("lat", "lon", None),
        P("lat", "lon", None, None),
        P("lat", "lon", None, None),
        P("lat", "lon", None),
        P("lat", "lon", None),
        P("lat", "lon"),
        P("lat", "lon", None),
        P("lat", "lon", None),
        P(None, "lat", "lon"),
        P(),
        P(),
        P(),
    )
    return jax.shard_map(
        on_device, mesh=mesh, in_specs=placed, out_specs=P("lat", "lon", None), check_vma=False
    )
```

```python
import jax
import jax.numpy as jnp
from jax import lax
from jax.experimental import pallas as pl
from jax.experimental.pallas import tpu as pltpu
from jax.sharding import PartitionSpec as P

L = 512
ROWS = 8
COLS = 128
MESH = 320
BORDER = 64
COARSE = 16
EDGE = 2560
G2M = 1536
ROUNDS = 2
CELLS = ROWS * COLS
N_LAT = 8
N_LON = 16
OUT = 18

NORTH, SOUTH, STRIPS = 1408, 1664, 1920
GRID_ROWS = 1632
NEAR_AT, COARSE_AT, WIDE = 640, 1152, 3200
DEC_OWN, DEC_WIDE = 384, 896

TILE = 512
EPSILON = 1e-05
F32 = jnp.float32
BF16 = jnp.bfloat16
NEIGHBOURS = [(p, q) for p in (-1, 0, 1) for q in (-1, 0, 1) if (p, q) != (0, 0)]
FAR_FIRST = sorted(
    ((i, j) for i in range(4) for j in range(4) if (i, j) != (0, 0)),
    key=lambda d: -min(d[0], 4 - d[0]) - min(d[1], 4 - d[1]),
)
XY = [(i, j, 0) for i, j in FAR_FIRST]
YZ = [(0, i, j) for i, j in FAR_FIRST]
PARTS = [(pl.ds(0, 256), "z", XY), (pl.ds(256, 256), "x", YZ)]


def tiles(count):
    return [pl.ds(t * TILE, TILE) for t in range(count // TILE)]


def dot(a, b):
    return jnp.dot(a, b, preferred_element_type=F32)


def hidden(before):
    half = 0.5 * before
    return (half + half * jnp.tanh(half)).astype(BF16)


def norm(result, gain):
    centre = jnp.sum(result, axis=-1, keepdims=True) * (1.0 / L)
    centred = result - centre
    spread = jnp.sum(centred * centred, axis=-1, keepdims=True) * (1.0 / L)
    return centred * lax.rsqrt(spread + EPSILON) * gain


def ones_where(mask):
    return jnp.where(mask, 1.0, 0.0).astype(BF16)


def short(value):
    return value.astype(jnp.int32).astype(jnp.int16)


def ones_where_short(mask):
    return jnp.where(mask, jnp.ones((), BF16), jnp.zeros((), BF16))


def steps_below(value, size, count):
    index = jnp.zeros_like(value)
    for step in range(1, count):
        index = index + jnp.where(value >= step * size, 1, 0)
    return index


def near_slot(source, own_at, near_at):
    block = steps_below(source, MESH, 9)
    row = source - block * MESH
    slot = block - jnp.where(block > 4, 1, 0)
    return jnp.where(block == 4, own_at + row, near_at + slot * BORDER + row)


def grid_slot(cell):
    r = steps_below(cell, COLS + 4, ROWS + 4)
    c = cell - r * (COLS + 4)
    north, south = r < 2, r >= ROWS + 2
    west, east = c < 2, c >= COLS + 2
    inside = (r - 2) * COLS + c - 2
    inside = jnp.where(north, NORTH + r * COLS + c - 2, inside)
    inside = jnp.where(south, SOUTH + (r - (ROWS + 2)) * COLS + c - 2, inside)
    strip = jnp.where(north, 2, jnp.where(south, 4, 0)) + jnp.where(east, 1, 0)
    strip_row = jnp.where(north, r + ROWS - 2, jnp.where(south, r - (ROWS + 2), r - 2))
    strip_col = jnp.where(east, c - (COLS + 2), c)
    side = STRIPS + strip * 16 + strip_row * 2 + strip_col
    return jnp.where(west | east, side, inside)


def edge_slot(source, core):
    far = source - 9 * MESH
    other = ((far >> 8) + core) & 1
    coarse = COARSE_AT + other * 1024 + (far >> 9) * 256 + (far & 255)
    return jnp.where(far >= 0, coarse, near_slot(source, 0, NEAR_AT))


def kernel(
    grid, mesh_in, edge_in, g2m_src, g2m_dst, g2m_count, mesh_src, mesh_dst, m2g_src,
    weights_in, weights_out, gains, out,
    w, cells, table, edges, acc, pick, place, coarse, near, proj, message, mesh_now, own_part, strips, square,
    local_sem, send_sem, recv_sem,
):
    lat, lon = lax.axis_index("lat"), lax.axis_index("lon")
    z, core = lax.div(lat, 2), lax.rem(lat, 2)
    x, y = lax.div(lon, 4), lax.rem(lon, 4)
    counts = {"local": 0, "remote": 0}

    def local(src, dst):
        i = counts["local"]
        counts["local"] += 1
        copy = pltpu.make_async_copy(src, dst, local_sem.at[i])
        copy.start()
        return copy

    def remote(src, dst, device):
        i = counts["remote"]
        counts["remote"] += 1
        copy = pltpu.make_async_remote_copy(
            src_ref=src, dst_ref=dst, send_sem=send_sem.at[i], recv_sem=recv_sem.at[i],
            device_id=device, device_id_type=pl.DeviceIdType.MESH,
        )
        copy.start()
        return copy

    def beside(p, q):
        return (lax.rem(lat + (p + N_LAT), N_LAT), lax.rem(lon + (q + N_LON), N_LON))

    def chip(dx, dy, dz):
        return (lax.rem(z + dz, 4) * 2 + core, lax.rem(x + dx, 4) * 4 + lax.rem(y + dy, 4))

    sibling = (z * 2 + (1 - core), lon)

    got_grid = local(grid, cells.at[pl.ds(0, CELLS)])
    got_weights = []
    for first, many, first_out, many_out in ((0, 4, 0, 2), (4, 5, 2, 2), (9, 5, 4, 2), (14, 4, 6, 2)):
        got_weights.append((
            local(weights_in.at[pl.ds(first, many)], w.at[pl.ds(first, many)]),
            local(weights_out.at[pl.ds(first_out, many_out)], w.at[pl.ds(OUT + first_out, many_out)]),
        ))
        if first == 0:
            got_edges = local(edge_in, edges)

    barrier = pltpu.get_barrier_semaphore()
    peers = [beside(p, q) for p, q in NEIGHBOURS] + [chip(*d) for d in sorted(set(XY + YZ))] + [sibling]
    for peer in peers:
        pl.semaphore_signal(barrier, inc=1, device_id=peer, device_id_type=pl.DeviceIdType.MESH)

    got_grid.wait()
    i = lax.broadcasted_iota(jnp.int32, (16, COLS), 0)
    j = lax.broadcasted_iota(jnp.int32, (16, COLS), 1)
    for side, first, shift in ((0, COLS - 16, 14), (1, 0, 0)):
        rim = jnp.concatenate([cells[r * COLS + first : r * COLS + first + 16] for r in range(ROWS)], axis=0)
        wanted = (i >> 1) * 16 + shift + (i & 1)
        strips[side] = dot(ones_where(j == wanted), rim).astype(BF16)

    pl.semaphore_wait(barrier, len(peers))
    halo = [
        remote(grid.at[pl.ds(CELLS - 256, 256)], cells.at[pl.ds(CELLS, 256)], beside(1, 0)),
        remote(grid.at[pl.ds(0, 256)], cells.at[pl.ds(CELLS + 256, 256)], beside(-1, 0)),
    ]
    for side, q in ((0, 1), (1, -1)):
        for place_at, p in ((0, 0), (2, 1), (4, -1)):
            to = CELLS + 512 + (place_at + side) * 16
            halo.append(remote(strips.at[side], cells.at[pl.ds(to, 16)], beside(p, q)))

    lanes = lax.broadcasted_iota(jnp.int32, (128, 128), 1).astype(jnp.int16)
    nodes = lax.broadcasted_iota(jnp.int32, (MESH, 128), 0)

    def stacked(ref):
        square[...] = jnp.zeros_like(square)
        many = ref.shape[1] // 128
        for t in range(many):
            square[t : t + 1, :] = ref[0:1, t * 128 : t * 128 + 128].astype(F32)
        return square[...].astype(jnp.int32), many

    def columns(index, many, at):
        turned = index.astype(F32).T
        for t in range(many):
            acc[t * 128 : t * 128 + 128, at : at + 128] = jnp.broadcast_to(turned[:, t : t + 1], (128, 128))

    source, many = stacked(g2m_src)
    columns(grid_slot(source), many, 0)
    target, many = stacked(g2m_dst)
    columns(target + CELLS, many, 128)

    @pl.loop(0, G2M // 128)
    def _(t):
        rows = pl.ds(pl.multiple_of(t * 128, 128), 128)
        first, second = short(acc[rows, 0:128]), short(acc[rows, 128:256])
        for chunk in range(16):
            ids = lanes + jnp.int16(chunk * 128)
            mask = (second if 8 <= chunk < 11 else first) == ids
            pick[rows, chunk * 128 : chunk * 128 + 128] = ones_where_short(mask)

    live = g2m_count[...]
    lane = lax.broadcasted_iota(jnp.int32, (1, 128), 1)
    for t in range(G2M // 128):
        target = jnp.where(lane + t * 128 < live, g2m_dst[0:1, t * 128 : t * 128 + 128], -1)
        place[:, EDGE + t * 128 : EDGE + t * 128 + 128] = ones_where(nodes == target)

    got_weights[0][0].wait()
    got_weights[0][1].wait()

    @pl.loop(0, CELLS // TILE)
    def _(t):
        rows = pl.ds(pl.multiple_of(t * TILE, TILE), TILE)
        table[rows, :] = dot(cells[rows, :], w[0]).astype(BF16)

    table[CELLS : CELLS + MESH] = dot(mesh_in[...], w[1]).astype(BF16)
    table[CELLS + MESH : NORTH] = jnp.zeros((NORTH - CELLS - MESH, L), BF16)
    table[NORTH + 608 :] = jnp.zeros((2048 - NORTH - 608, L), BF16)
    own_part[...] = dot(mesh_in[...], w[2])

    @pl.loop(0, G2M // TILE)
    def _(t):
        rows = pl.ds(pl.multiple_of(t * TILE, TILE), TILE)
        acc[rows, :] = dot(pick[rows, 0:NORTH], table[0:NORTH])

    for copy in halo:
        copy.wait_recv()
    table[NORTH : NORTH + 608] = dot(cells[CELLS:GRID_ROWS], w[0]).astype(BF16)

    for rows in tiles(G2M):
        before = acc[rows, :] + dot(pick[rows, NORTH:2048], table[NORTH:2048])
        message[rows, :] = norm(dot(hidden(before), w[OUT]), gains[0:1, :]).astype(BF16)

    def new_nodes(old, self_part, totals, second, k):
        before = self_part + dot(totals.astype(BF16), w[second])
        return (old.astype(F32) + norm(dot(hidden(before), w[OUT + k]), gains[k : k + 1, :])).astype(BF16)

    def update_encoded(a, b):
        totals = dot(place[a:b, EDGE : EDGE + G2M], message[...])
        mesh_now[a:b] = new_nodes(mesh_in[a:b], own_part[a:b], totals, 3, 1)

    def update_round(r):
        def update(a, b):
            totals = dot(place[a:b, 0:EDGE], edges[...])
            mesh_now[a:b] = new_nodes(mesh_now[a:b], own_part[a:b], totals, 8 + 5 * r, 3 + 2 * r)

        return update

    sent = list(halo)

    def send_near(r):
        copies = []
        for slot, (p, q) in enumerate(NEIGHBOURS):
            copies.append(remote(proj.at[r, pl.ds(0, BORDER)], near.at[r, slot], beside(-p, -q)))
        sent.extend(copies)
        return copies

    def plane(r, part, axis, d):
        here = lax.rem({"x": x, "z": z}[axis] + (4 - d), 4)
        if axis == "z":
            return coarse.at[r, 0, here, :, :, :, part]
        return coarse.at[r, 0, :, here, :, :, part]

    update = update_encoded
    for r in range(ROUNDS):
        first = 4 + 5 * r
        got_weights[1 + r][0].wait()
        got_weights[1 + r][1].wait()
        update(MESH - COARSE, MESH)
        coarse[r, 0, z, x, y] = dot(mesh_now[MESH - COARSE : MESH], w[first + 1]).astype(BF16)
        arriving = []
        for part, axis, offsets in PARTS:
            ref = coarse.at[r, 0, z, x, y, :, part]
            arriving.append([remote(ref, ref, chip(*d)) for d in offsets])
            sent.extend(arriving[-1])
        update(0, MESH - COARSE)
        proj[r, 0:MESH] = dot(mesh_now[...], w[first + 1]).astype(BF16)
        got_near = send_near(r)
        proj[r, MESH : 2 * MESH] = dot(mesh_now[...], w[first + 2]).astype(BF16)
        own_part[...] = dot(mesh_now[...], w[first + 3])

        if r == 0:
            got_edges.wait()
            source, many = stacked(mesh_src)
            columns(edge_slot(source, core), many, 0)
            target, many = stacked(mesh_dst)
            columns(target + MESH, many, 128)

        across = []

        def second_stage():
            moving = []
            for k, (part, axis, offsets) in enumerate(PARTS):
                for copy in arriving[k]:
                    copy.wait_recv()
                ref = plane(r, part, axis, 0)
                moving.append([
                    remote(ref, ref, chip(**{"dx": 0, "dy": 0, "dz": 0, "d" + axis: d})) for d in (1, 2, 3)
                ])
                sent.extend(moving[-1])
            for part, axis, offsets in PARTS:
                across.append(forward(part, axis, 0))
            return moving

        def forward(part, axis, d):
            here = lax.rem({"x": x, "z": z}[axis] + (4 - d), 4)
            if axis == "z":
                return remote(
                    coarse.at[r, 0, here, :, :, :, part], coarse.at[r, 1, here, :, :, :, part], sibling
                )
            return remote(
                coarse.at[r, 0, :, here, :, :, part], coarse.at[r, 1, :, here, :, :, part], sibling
            )

        if r == 0:
            moving = second_stage()

            @pl.loop(0, EDGE // 128)
            def _(t):
                rows = pl.ds(pl.multiple_of(t * 128, 128), 128)
                one, two = short(acc[rows, 0:128]), short(acc[rows, 128:256])
                for chunk in range(WIDE // 128):
                    ids = lanes + jnp.int16(chunk * 128)
                    if chunk in (3, 4):
                        mask = two == ids
                    elif chunk == 2:
                        mask = (one == ids) | (two == ids)
                    else:
                        mask = one == ids
                    pick[rows, chunk * 128 : chunk * 128 + 128] = ones_where_short(mask)

            for t in range(EDGE // 128):
                place[:, t * 128 : t * 128 + 128] = ones_where(nodes == mesh_dst[0:1, t * 128 : t * 128 + 128])

        if r == 0:
            for copy in got_near:
                copy.wait_recv()
            for rows in tiles(EDGE):
                acc[rows, :] = (
                    dot(edges[rows, :], w[first])
                    + dot(pick[rows, 0:NEAR_AT], proj[r])
                    + dot(pick[rows, NEAR_AT:COARSE_AT], near[r].reshape(8 * BORDER, L))
                )
        else:
            for rows in tiles(EDGE):
                acc[rows, :] = dot(edges[rows, :], w[first]) + dot(pick[rows, 0:NEAR_AT], proj[r])
            moving = second_stage()
            for copy in got_near:
                copy.wait_recv()
            for rows in tiles(EDGE):
                acc[rows, :] += dot(pick[rows, NEAR_AT:COARSE_AT], near[r].reshape(8 * BORDER, L))

        for d in (1, 2, 3):
            for k, (part, axis, offsets) in enumerate(PARTS):
                moving[k][d - 1].wait_recv()
                across.append(forward(part, axis, d))
        sent.extend(across)

        for rows in tiles(EDGE):
            acc[rows, :] += dot(pick[rows, COARSE_AT : COARSE_AT + 1024], coarse[r, 0].reshape(1024, L))

        for copy in across:
            copy.wait_recv()

        for rows in tiles(EDGE):
            before = acc[rows, :] + dot(pick[rows, COARSE_AT + 1024 : WIDE], coarse[r, 1].reshape(1024, L))
            result = norm(dot(hidden(before), w[OUT + 2 + 2 * r]), gains[2 + 2 * r : 3 + 2 * r, :])
            edges[rows, :] = (edges[rows, :].astype(F32) + result).astype(BF16)

        update = update_round(r)

    got_weights[3][0].wait()
    got_weights[3][1].wait()
    update(0, BORDER)
    proj[ROUNDS, 0:BORDER] = dot(mesh_now[0:BORDER], w[14]).astype(BF16)
    got_near = send_near(ROUNDS)
    update(BORDER, MESH)
    proj[ROUNDS, BORDER:MESH] = dot(mesh_now[BORDER:MESH], w[14]).astype(BF16)
    proj[ROUNDS, MESH : 2 * MESH] = jnp.zeros((MESH, L), BF16)

    square[...] = jnp.zeros_like(square)
    square[0:24] = m2g_src[...].astype(F32)
    columns(near_slot(square[...].astype(jnp.int32), 0, DEC_OWN), 24, 0)

    @pl.loop(0, ROWS)
    def _(t):
        to = pl.ds(pl.multiple_of(t * 128, 128), 128)
        for corner in range(3):
            one = short(acc[pl.ds(pl.multiple_of(corner * CELLS + t * 128, 128), 128), 0:128])
            for chunk in range(DEC_WIDE // 128):
                at = corner * DEC_WIDE + chunk * 128
                pick[to, at : at + 128] = ones_where_short(one == lanes + jnp.int16(chunk * 128))

    @pl.loop(0, CELLS // TILE)
    def _(t):
        rows = pl.ds(pl.multiple_of(t * TILE, TILE), TILE)
        base = dot(cells[rows, :], w[15])
        for corner in range(3):
            at = corner * DEC_WIDE
            to = pl.ds(pl.multiple_of(corner * CELLS + t * TILE, TILE), TILE)
            acc[to, :] = base + dot(pick[rows, at : at + DEC_OWN], proj[ROUNDS, 0:DEC_OWN])

    for copy in got_near:
        copy.wait_recv()

    for t, rows in enumerate(tiles(CELLS)):
        totals = jnp.zeros((TILE, L), F32)
        for corner in range(3):
            at = corner * DEC_WIDE
            to = pl.ds(corner * CELLS + t * TILE, TILE)
            before = acc[to, :] + dot(
                pick[rows, at + DEC_OWN : at + DEC_WIDE], near[ROUNDS].reshape(8 * BORDER, L)
            )
            totals = totals + norm(dot(hidden(before), w[OUT + 6]), gains[6:7, :])
        out[rows, :] = new_nodes(cells[rows, :], dot(cells[rows, :], w[16]), totals, 17, 7)

    for copy in sent:
        copy.wait_send()


def on_device(
    grid_latent, mesh_latent, edge_latent, g2m_src, g2m_dst, g2m_count, mesh_src, mesh_dst, m2g_src,
    weights_in, weights_out, gains,
):
    anywhere = pl.BlockSpec(memory_space=pl.ANY)
    vmem = pl.BlockSpec(memory_space=pltpu.VMEM)
    result = pl.pallas_call(
        kernel,
        out_shape=jax.ShapeDtypeStruct((CELLS, L), BF16),
        in_specs=[anywhere, vmem, anywhere] + [vmem] * 6 + [anywhere, anywhere, vmem],
        out_specs=vmem,
        scratch_shapes=[
            pltpu.VMEM((26, L, L), BF16),
            pltpu.VMEM((GRID_ROWS, L), BF16),
            pltpu.VMEM((2048, L), BF16),
            pltpu.VMEM((EDGE, L), BF16),
            pltpu.VMEM((3 * CELLS, L), F32),
            pltpu.VMEM((EDGE, WIDE), BF16),
            pltpu.VMEM((MESH, EDGE + G2M), BF16),
            pltpu.VMEM((ROUNDS, 2, 4, 4, 4, COARSE, L), BF16),
            pltpu.VMEM((ROUNDS + 1, 8, BORDER, L), BF16),
            pltpu.VMEM((ROUNDS + 1, 2 * MESH, L), BF16),
            pltpu.VMEM((G2M, L), BF16),
            pltpu.VMEM((MESH, L), BF16),
            pltpu.VMEM((MESH, L), F32),
            pltpu.VMEM((2, 16, L), BF16),
            pltpu.VMEM((128, 128), F32),
            pltpu.SemaphoreType.DMA((10,)),
            pltpu.SemaphoreType.DMA((120,)),
            pltpu.SemaphoreType.DMA((120,)),
        ],
        compiler_params=pltpu.CompilerParams(
            collective_id=0, has_side_effects=True, vmem_limit_bytes=62 * 1024 * 1024
        ),
        cost_estimate=pl.CostEstimate(flops=40_000_000_000, bytes_accessed=20_000_000, transcendentals=10_000_000),
    )(
        grid_latent.reshape(CELLS, L), mesh_latent.reshape(MESH, L), edge_latent.reshape(EDGE, L),
        g2m_src.reshape(1, G2M), g2m_dst.reshape(1, G2M), g2m_count,
        mesh_src.reshape(1, EDGE), mesh_dst.reshape(1, EDGE), m2g_src.reshape(-1, 128),
        weights_in, weights_out, gains,
    )
    return result.reshape(grid_latent.shape)


def solution(mesh):
    placed = (
        P("lat", "lon", None),
        P("lat", "lon", None, None),
        P("lat", "lon", None, None),
        P("lat", "lon", None),
        P("lat", "lon", None),
        P("lat", "lon"),
        P("lat", "lon", None),
        P("lat", "lon", None),
        P(None, "lat", "lon"),
        P(),
        P(),
        P(),
    )
    return jax.shard_map(
        on_device, mesh=mesh, in_specs=placed, out_specs=P("lat", "lon", None), check_vma=False
    )
```

```python
import jax
import jax.numpy as jnp
from jax import lax
from jax.experimental import pallas as pl
from jax.experimental.pallas import tpu as pltpu
from jax.sharding import PartitionSpec as P

L = 512
ROWS = 8
COLS = 128
MESH = 320
BORDER = 64
COARSE = 16
EDGE = 2560
G2M = 1536
ROUNDS = 2
CELLS = ROWS * COLS
N_LAT = 8
N_LON = 16
OUT = 18

NORTH, SOUTH, STRIPS = 1408, 1664, 1920
GRID_ROWS = 1632
NEAR_AT, COARSE_AT, WIDE = 640, 1152, 3200
DEC_OWN, DEC_WIDE = 384, 896

TILE = 512
EPSILON = 1e-05
F32 = jnp.float32
BF16 = jnp.bfloat16
NEIGHBOURS = [(p, q) for p in (-1, 0, 1) for q in (-1, 0, 1) if (p, q) != (0, 0)]
FAR_FIRST = sorted(
    ((i, j) for i in range(4) for j in range(4) if (i, j) != (0, 0)),
    key=lambda d: -min(d[0], 4 - d[0]) - min(d[1], 4 - d[1]),
)
XY = [(i, j, 0) for i, j in FAR_FIRST]
YZ = [(0, i, j) for i, j in FAR_FIRST]
PARTS = [(pl.ds(0, 256), "z", XY), (pl.ds(256, 256), "x", YZ)]


def tiles(count):
    return [pl.ds(t * TILE, TILE) for t in range(count // TILE)]


def dot(a, b):
    return jnp.dot(a, b, preferred_element_type=F32)


def hidden(before):
    half = 0.5 * before
    return (half + half * jnp.tanh(half)).astype(BF16)


def norm(result, gain):
    centre = jnp.sum(result, axis=-1, keepdims=True) * (1.0 / L)
    centred = result - centre
    spread = jnp.sum(centred * centred, axis=-1, keepdims=True) * (1.0 / L)
    return centred * lax.rsqrt(spread + EPSILON) * gain


def ones_where(mask):
    return jnp.where(mask, 1.0, 0.0).astype(BF16)


def short(value):
    return value.astype(jnp.int32).astype(jnp.int16)


def ones_where_short(mask):
    return jnp.where(mask, jnp.ones((), BF16), jnp.zeros((), BF16))


def steps_below(value, size, count):
    index = jnp.zeros_like(value)
    for step in range(1, count):
        index = index + jnp.where(value >= step * size, 1, 0)
    return index


def near_slot(source, own_at, near_at):
    block = steps_below(source, MESH, 9)
    row = source - block * MESH
    slot = block - jnp.where(block > 4, 1, 0)
    return jnp.where(block == 4, own_at + row, near_at + slot * BORDER + row)


def grid_slot(cell):
    r = steps_below(cell, COLS + 4, ROWS + 4)
    c = cell - r * (COLS + 4)
    north, south = r < 2, r >= ROWS + 2
    west, east = c < 2, c >= COLS + 2
    inside = (r - 2) * COLS + c - 2
    inside = jnp.where(north, NORTH + r * COLS + c - 2, inside)
    inside = jnp.where(south, SOUTH + (r - (ROWS + 2)) * COLS + c - 2, inside)
    strip = jnp.where(north, 2, jnp.where(south, 4, 0)) + jnp.where(east, 1, 0)
    strip_row = jnp.where(north, r + ROWS - 2, jnp.where(south, r - (ROWS + 2), r - 2))
    strip_col = jnp.where(east, c - (COLS + 2), c)
    side = STRIPS + strip * 16 + strip_row * 2 + strip_col
    return jnp.where(west | east, side, inside)


def edge_slot(source, core):
    far = source - 9 * MESH
    other = ((far >> 8) + core) & 1
    coarse = COARSE_AT + other * 1024 + (far >> 9) * 256 + (far & 255)
    return jnp.where(far >= 0, coarse, near_slot(source, 0, NEAR_AT))


def kernel(
    grid, mesh_in, edge_in, g2m_src, g2m_dst, g2m_count, mesh_src, mesh_dst, m2g_src,
    weights_in, weights_out, gains, out,
    w, cells, table, edges, acc, pick, place, coarse, near, proj, message, mesh_now, own_part, strips, square,
    local_sem, send_sem, recv_sem,
):
    lat, lon = lax.axis_index("lat"), lax.axis_index("lon")
    z, core = lax.div(lat, 2), lax.rem(lat, 2)
    x, y = lax.div(lon, 4), lax.rem(lon, 4)
    counts = {"local": 0, "remote": 0}

    def local(src, dst):
        i = counts["local"]
        counts["local"] += 1
        copy = pltpu.make_async_copy(src, dst, local_sem.at[i])
        copy.start()
        return copy

    def remote(src, dst, device):
        i = counts["remote"]
        counts["remote"] += 1
        copy = pltpu.make_async_remote_copy(
            src_ref=src, dst_ref=dst, send_sem=send_sem.at[i], recv_sem=recv_sem.at[i],
            device_id=device, device_id_type=pl.DeviceIdType.MESH,
        )
        copy.start()
        return copy

    def beside(p, q):
        return (lax.rem(lat + (p + N_LAT), N_LAT), lax.rem(lon + (q + N_LON), N_LON))

    def chip(dx, dy, dz):
        return (lax.rem(z + dz, 4) * 2 + core, lax.rem(x + dx, 4) * 4 + lax.rem(y + dy, 4))

    sibling = (z * 2 + (1 - core), lon)

    got_grid = local(grid, cells.at[pl.ds(0, CELLS)])
    got_weights = []
    for first, many, first_out, many_out in ((0, 4, 0, 2), (4, 5, 2, 2), (9, 5, 4, 2), (14, 4, 6, 2)):
        got_weights.append((
            local(weights_in.at[pl.ds(first, many)], w.at[pl.ds(first, many)]),
            local(weights_out.at[pl.ds(first_out, many_out)], w.at[pl.ds(OUT + first_out, many_out)]),
        ))
        if first == 0:
            got_edges = local(edge_in, edges)

    barrier = pltpu.get_barrier_semaphore()
    peers = [beside(p, q) for p, q in NEIGHBOURS] + [chip(*d) for d in sorted(set(XY + YZ))] + [sibling]
    for peer in peers:
        pl.semaphore_signal(barrier, inc=1, device_id=peer, device_id_type=pl.DeviceIdType.MESH)

    got_grid.wait()
    i = lax.broadcasted_iota(jnp.int32, (16, COLS), 0)
    j = lax.broadcasted_iota(jnp.int32, (16, COLS), 1)
    for side, first, shift in ((0, COLS - 16, 14), (1, 0, 0)):
        rim = jnp.concatenate([cells[r * COLS + first : r * COLS + first + 16] for r in range(ROWS)], axis=0)
        wanted = (i >> 1) * 16 + shift + (i & 1)
        strips[side] = dot(ones_where(j == wanted), rim).astype(BF16)

    pl.semaphore_wait(barrier, len(peers))
    halo = [
        remote(grid.at[pl.ds(CELLS - 256, 256)], cells.at[pl.ds(CELLS, 256)], beside(1, 0)),
        remote(grid.at[pl.ds(0, 256)], cells.at[pl.ds(CELLS + 256, 256)], beside(-1, 0)),
    ]
    for side, q in ((0, 1), (1, -1)):
        for place_at, p in ((0, 0), (2, 1), (4, -1)):
            to = CELLS + 512 + (place_at + side) * 16
            halo.append(remote(strips.at[side], cells.at[pl.ds(to, 16)], beside(p, q)))

    lanes = lax.broadcasted_iota(jnp.int32, (128, 128), 1).astype(jnp.int16)
    nodes = lax.broadcasted_iota(jnp.int32, (MESH, 128), 0)

    def stacked(ref):
        square[...] = jnp.zeros_like(square)
        many = ref.shape[1] // 128
        for t in range(many):
            square[t : t + 1, :] = ref[0:1, t * 128 : t * 128 + 128].astype(F32)
        return square[...].astype(jnp.int32), many

    def columns(index, many, at):
        turned = index.astype(F32).T
        for t in range(many):
            acc[t * 128 : t * 128 + 128, at : at + 128] = jnp.broadcast_to(turned[:, t : t + 1], (128, 128))

    source, many = stacked(g2m_src)
    columns(grid_slot(source), many, 0)
    target, many = stacked(g2m_dst)
    columns(target + CELLS, many, 128)

    @pl.loop(0, G2M // 128)
    def _(t):
        rows = pl.ds(pl.multiple_of(t * 128, 128), 128)
        first, second = short(acc[rows, 0:128]), short(acc[rows, 128:256])
        for chunk in range(16):
            ids = lanes + jnp.int16(chunk * 128)
            mask = (second if 8 <= chunk < 11 else first) == ids
            pick[rows, chunk * 128 : chunk * 128 + 128] = ones_where_short(mask)

    live = g2m_count[...]
    lane = lax.broadcasted_iota(jnp.int32, (1, 128), 1)
    for t in range(G2M // 128):
        target = jnp.where(lane + t * 128 < live, g2m_dst[0:1, t * 128 : t * 128 + 128], -1)
        place[:, EDGE + t * 128 : EDGE + t * 128 + 128] = ones_where(nodes == target)

    got_weights[0][0].wait()
    got_weights[0][1].wait()

    @pl.loop(0, CELLS // TILE)
    def _(t):
        rows = pl.ds(pl.multiple_of(t * TILE, TILE), TILE)
        table[rows, :] = dot(cells[rows, :], w[0]).astype(BF16)

    table[CELLS : CELLS + MESH] = dot(mesh_in[...], w[1]).astype(BF16)
    table[CELLS + MESH : NORTH] = jnp.zeros((NORTH - CELLS - MESH, L), BF16)
    table[NORTH + 608 :] = jnp.zeros((2048 - NORTH - 608, L), BF16)
    own_part[...] = dot(mesh_in[...], w[2])

    @pl.loop(0, G2M // TILE)
    def _(t):
        rows = pl.ds(pl.multiple_of(t * TILE, TILE), TILE)
        acc[rows, :] = dot(pick[rows, 0:NORTH], table[0:NORTH])

    for copy in halo:
        copy.wait_recv()
    table[NORTH : NORTH + 608] = dot(cells[CELLS:GRID_ROWS], w[0]).astype(BF16)

    for rows in tiles(G2M):
        before = acc[rows, :] + dot(pick[rows, NORTH:2048], table[NORTH:2048])
        message[rows, :] = norm(dot(hidden(before), w[OUT]), gains[0:1, :]).astype(BF16)

    def new_nodes(old, self_part, totals, second, k):
        before = self_part + dot(totals.astype(BF16), w[second])
        return (old.astype(F32) + norm(dot(hidden(before), w[OUT + k]), gains[k : k + 1, :])).astype(BF16)

    def update_encoded(a, b):
        totals = dot(place[a:b, EDGE : EDGE + G2M], message[...])
        mesh_now[a:b] = new_nodes(mesh_in[a:b], own_part[a:b], totals, 3, 1)

    def update_round(r):
        def update(a, b):
            totals = dot(place[a:b, 0:EDGE], edges[...])
            mesh_now[a:b] = new_nodes(mesh_now[a:b], own_part[a:b], totals, 8 + 5 * r, 3 + 2 * r)

        return update

    sent = list(halo)

    def send_near(r):
        copies = []
        for slot, (p, q) in enumerate(NEIGHBOURS):
            copies.append(remote(proj.at[r, pl.ds(0, BORDER)], near.at[r, slot], beside(-p, -q)))
        sent.extend(copies)
        return copies

    def plane(r, part, axis, d):
        here = lax.rem({"x": x, "z": z}[axis] + (4 - d), 4)
        if axis == "z":
            return coarse.at[r, 0, here, :, :, :, part]
        return coarse.at[r, 0, :, here, :, :, part]

    update = update_encoded
    for r in range(ROUNDS):
        first = 4 + 5 * r
        got_weights[1 + r][0].wait()
        got_weights[1 + r][1].wait()
        update(MESH - COARSE, MESH)
        coarse[r, 0, z, x, y] = dot(mesh_now[MESH - COARSE : MESH], w[first + 1]).astype(BF16)
        arriving = []
        for part, axis, offsets in PARTS:
            ref = coarse.at[r, 0, z, x, y, :, part]
            arriving.append([remote(ref, ref, chip(*d)) for d in offsets])
            sent.extend(arriving[-1])
        update(0, MESH - COARSE)
        proj[r, 0:MESH] = dot(mesh_now[...], w[first + 1]).astype(BF16)
        got_near = send_near(r)
        proj[r, MESH : 2 * MESH] = dot(mesh_now[...], w[first + 2]).astype(BF16)
        own_part[...] = dot(mesh_now[...], w[first + 3])

        if r == 0:
            got_edges.wait()
            source, many = stacked(mesh_src)
            columns(edge_slot(source, core), many, 0)
            target, many = stacked(mesh_dst)
            columns(target + MESH, many, 128)

        across = []

        def second_stage():
            moving = []
            for k, (part, axis, offsets) in enumerate(PARTS):
                for copy in arriving[k]:
                    copy.wait_recv()
                ref = plane(r, part, axis, 0)
                moving.append([
                    remote(ref, ref, chip(**{"dx": 0, "dy": 0, "dz": 0, "d" + axis: d})) for d in (1, 2, 3)
                ])
                sent.extend(moving[-1])
            for part, axis, offsets in PARTS:
                across.append(forward(part, axis, 0))
            return moving

        def forward(part, axis, d):
            here = lax.rem({"x": x, "z": z}[axis] + (4 - d), 4)
            if axis == "z":
                return remote(
                    coarse.at[r, 0, here, :, :, :, part], coarse.at[r, 1, here, :, :, :, part], sibling
                )
            return remote(
                coarse.at[r, 0, :, here, :, :, part], coarse.at[r, 1, :, here, :, :, part], sibling
            )

        if r == 0:
            moving = second_stage()

            @pl.loop(0, EDGE // 128)
            def _(t):
                rows = pl.ds(pl.multiple_of(t * 128, 128), 128)
                one, two = short(acc[rows, 0:128]), short(acc[rows, 128:256])
                for chunk in range(WIDE // 128):
                    ids = lanes + jnp.int16(chunk * 128)
                    if chunk in (3, 4):
                        mask = two == ids
                    elif chunk == 2:
                        mask = (one == ids) | (two == ids)
                    else:
                        mask = one == ids
                    pick[rows, chunk * 128 : chunk * 128 + 128] = ones_where_short(mask)

            for t in range(EDGE // 128):
                place[:, t * 128 : t * 128 + 128] = ones_where(nodes == mesh_dst[0:1, t * 128 : t * 128 + 128])

        if r == 0:
            for copy in got_near:
                copy.wait_recv()
            for rows in tiles(EDGE):
                acc[rows, :] = (
                    dot(edges[rows, :], w[first])
                    + dot(pick[rows, 0:NEAR_AT], proj[r])
                    + dot(pick[rows, NEAR_AT:COARSE_AT], near[r].reshape(8 * BORDER, L))
                )
        else:
            for rows in tiles(EDGE):
                acc[rows, :] = dot(edges[rows, :], w[first]) + dot(pick[rows, 0:NEAR_AT], proj[r])
            moving = second_stage()
            for copy in got_near:
                copy.wait_recv()
            for rows in tiles(EDGE):
                acc[rows, :] += dot(pick[rows, NEAR_AT:COARSE_AT], near[r].reshape(8 * BORDER, L))

        for d in (1, 2, 3):
            for k, (part, axis, offsets) in enumerate(PARTS):
                moving[k][d - 1].wait_recv()
                across.append(forward(part, axis, d))
        sent.extend(across)

        for rows in tiles(EDGE):
            acc[rows, :] += dot(pick[rows, COARSE_AT : COARSE_AT + 1024], coarse[r, 0].reshape(1024, L))

        for copy in across:
            copy.wait_recv()

        for rows in tiles(EDGE):
            before = acc[rows, :] + dot(pick[rows, COARSE_AT + 1024 : WIDE], coarse[r, 1].reshape(1024, L))
            result = norm(dot(hidden(before), w[OUT + 2 + 2 * r]), gains[2 + 2 * r : 3 + 2 * r, :])
            edges[rows, :] = (edges[rows, :].astype(F32) + result).astype(BF16)

        update = update_round(r)

    got_weights[3][0].wait()
    got_weights[3][1].wait()
    update(0, BORDER)
    proj[ROUNDS, 0:BORDER] = dot(mesh_now[0:BORDER], w[14]).astype(BF16)
    got_near = send_near(ROUNDS)
    update(BORDER, MESH)
    proj[ROUNDS, BORDER:MESH] = dot(mesh_now[BORDER:MESH], w[14]).astype(BF16)
    proj[ROUNDS, MESH : 2 * MESH] = jnp.zeros((MESH, L), BF16)

    square[...] = jnp.zeros_like(square)
    square[0:24] = m2g_src[...].astype(F32)
    columns(near_slot(square[...].astype(jnp.int32), 0, DEC_OWN), 24, 0)

    @pl.loop(0, ROWS)
    def _(t):
        to = pl.ds(pl.multiple_of(t * 128, 128), 128)
        for corner in range(3):
            one = short(acc[pl.ds(pl.multiple_of(corner * CELLS + t * 128, 128), 128), 0:128])
            for chunk in range(DEC_WIDE // 128):
                at = corner * DEC_WIDE + chunk * 128
                pick[to, at : at + 128] = ones_where_short(one == lanes + jnp.int16(chunk * 128))

    @pl.loop(0, CELLS // TILE)
    def _(t):
        rows = pl.ds(pl.multiple_of(t * TILE, TILE), TILE)
        base = dot(cells[rows, :], w[15])
        for corner in range(3):
            at = corner * DEC_WIDE
            to = pl.ds(pl.multiple_of(corner * CELLS + t * TILE, TILE), TILE)
            acc[to, :] = base + dot(pick[rows, at : at + DEC_OWN], proj[ROUNDS, 0:DEC_OWN])

    for copy in got_near:
        copy.wait_recv()

    @pl.loop(0, CELLS // TILE)
    def _(t):
        rows = pl.ds(pl.multiple_of(t * TILE, TILE), TILE)
        totals = jnp.zeros((TILE, L), F32)
        for corner in range(3):
            at = corner * DEC_WIDE
            to = pl.ds(pl.multiple_of(corner * CELLS + t * TILE, TILE), TILE)
            before = acc[to, :] + dot(
                pick[rows, at + DEC_OWN : at + DEC_WIDE], near[ROUNDS].reshape(8 * BORDER, L)
            )
            totals = totals + norm(dot(hidden(before), w[OUT + 6]), gains[6:7, :])
        out[rows, :] = new_nodes(cells[rows, :], dot(cells[rows, :], w[16]), totals, 17, 7)

    for copy in sent:
        copy.wait_send()


def on_device(
    grid_latent, mesh_latent, edge_latent, g2m_src, g2m_dst, g2m_count, mesh_src, mesh_dst, m2g_src,
    weights_in, weights_out, gains,
):
    anywhere = pl.BlockSpec(memory_space=pl.ANY)
    vmem = pl.BlockSpec(memory_space=pltpu.VMEM)
    result = pl.pallas_call(
        kernel,
        out_shape=jax.ShapeDtypeStruct((CELLS, L), BF16),
        in_specs=[anywhere, vmem, anywhere] + [vmem] * 6 + [anywhere, anywhere, vmem],
        out_specs=vmem,
        scratch_shapes=[
            pltpu.VMEM((26, L, L), BF16),
            pltpu.VMEM((GRID_ROWS, L), BF16),
            pltpu.VMEM((2048, L), BF16),
            pltpu.VMEM((EDGE, L), BF16),
            pltpu.VMEM((3 * CELLS, L), F32),
            pltpu.VMEM((EDGE, WIDE), BF16),
            pltpu.VMEM((MESH, EDGE + G2M), BF16),
            pltpu.VMEM((ROUNDS, 2, 4, 4, 4, COARSE, L), BF16),
            pltpu.VMEM((ROUNDS + 1, 8, BORDER, L), BF16),
            pltpu.VMEM((ROUNDS + 1, 2 * MESH, L), BF16),
            pltpu.VMEM((G2M, L), BF16),
            pltpu.VMEM((MESH, L), BF16),
            pltpu.VMEM((MESH, L), F32),
            pltpu.VMEM((2, 16, L), BF16),
            pltpu.VMEM((128, 128), F32),
            pltpu.SemaphoreType.DMA((10,)),
            pltpu.SemaphoreType.DMA((120,)),
            pltpu.SemaphoreType.DMA((120,)),
        ],
        compiler_params=pltpu.CompilerParams(
            collective_id=0, has_side_effects=True, vmem_limit_bytes=62 * 1024 * 1024
        ),
        cost_estimate=pl.CostEstimate(flops=40_000_000_000, bytes_accessed=20_000_000, transcendentals=10_000_000),
    )(
        grid_latent.reshape(CELLS, L), mesh_latent.reshape(MESH, L), edge_latent.reshape(EDGE, L),
        g2m_src.reshape(1, G2M), g2m_dst.reshape(1, G2M), g2m_count,
        mesh_src.reshape(1, EDGE), mesh_dst.reshape(1, EDGE), m2g_src.reshape(-1, 128),
        weights_in, weights_out, gains,
    )
    return result.reshape(grid_latent.shape)


def solution(mesh):
    placed = (
        P("lat", "lon", None),
        P("lat", "lon", None, None),
        P("lat", "lon", None, None),
        P("lat", "lon", None),
        P("lat", "lon", None),
        P("lat", "lon"),
        P("lat", "lon", None),
        P("lat", "lon", None),
        P(None, "lat", "lon"),
        P(),
        P(),
        P(),
    )
    return jax.shard_map(
        on_device, mesh=mesh, in_specs=placed, out_specs=P("lat", "lon", None), check_vma=False
    )
```

```python
import jax
import jax.numpy as jnp
from jax import lax
from jax.experimental import pallas as pl
from jax.experimental.pallas import tpu as pltpu
from jax.sharding import PartitionSpec as P

L = 512
ROWS = 8
COLS = 128
MESH = 320
BORDER = 64
COARSE = 16
EDGE = 2560
G2M = 1536
ROUNDS = 2
CELLS = ROWS * COLS
N_LAT = 8
N_LON = 16
OUT = 18

NORTH, SOUTH, STRIPS = 1408, 1664, 1920
GRID_ROWS = 1632
NEAR_AT, COARSE_AT, WIDE = 640, 1152, 3200
DEC_OWN, DEC_WIDE = 384, 896

TILE = 512
EPSILON = 1e-05
F32 = jnp.float32
BF16 = jnp.bfloat16
NEIGHBOURS = [(p, q) for p in (-1, 0, 1) for q in (-1, 0, 1) if (p, q) != (0, 0)]
FAR_FIRST = sorted(
    ((i, j) for i in range(4) for j in range(4) if (i, j) != (0, 0)),
    key=lambda d: -min(d[0], 4 - d[0]) - min(d[1], 4 - d[1]),
)
XY = [(i, j, 0) for i, j in FAR_FIRST]
YZ = [(0, i, j) for i, j in FAR_FIRST]
PARTS = [(pl.ds(0, 256), "z", XY), (pl.ds(256, 256), "x", YZ)]


def tiles(count):
    return [pl.ds(t * TILE, TILE) for t in range(count // TILE)]


def dot(a, b):
    return jnp.dot(a, b, preferred_element_type=F32)


def hidden(before):
    half = 0.5 * before
    return (half + half * jnp.tanh(half)).astype(BF16)


def norm(result, gain):
    centre = jnp.sum(result, axis=-1, keepdims=True) * (1.0 / L)
    centred = result - centre
    spread = jnp.sum(centred * centred, axis=-1, keepdims=True) * (1.0 / L)
    return centred * lax.rsqrt(spread + EPSILON) * gain


def ones_where(mask):
    return jnp.where(mask, 1.0, 0.0).astype(BF16)


def short(value):
    return value.astype(jnp.int32).astype(jnp.int16)


def ones_where_short(mask):
    return jnp.where(mask, jnp.ones((), BF16), jnp.zeros((), BF16))


def steps_below(value, size, count):
    index = jnp.zeros_like(value)
    for step in range(1, count):
        index = index + jnp.where(value >= step * size, 1, 0)
    return index


def near_slot(source, own_at, near_at):
    block = steps_below(source, MESH, 9)
    row = source - block * MESH
    slot = block - jnp.where(block > 4, 1, 0)
    return jnp.where(block == 4, own_at + row, near_at + slot * BORDER + row)


def grid_slot(cell):
    r = steps_below(cell, COLS + 4, ROWS + 4)
    c = cell - r * (COLS + 4)
    north, south = r < 2, r >= ROWS + 2
    west, east = c < 2, c >= COLS + 2
    inside = (r - 2) * COLS + c - 2
    inside = jnp.where(north, NORTH + r * COLS + c - 2, inside)
    inside = jnp.where(south, SOUTH + (r - (ROWS + 2)) * COLS + c - 2, inside)
    strip = jnp.where(north, 2, jnp.where(south, 4, 0)) + jnp.where(east, 1, 0)
    strip_row = jnp.where(north, r + ROWS - 2, jnp.where(south, r - (ROWS + 2), r - 2))
    strip_col = jnp.where(east, c - (COLS + 2), c)
    side = STRIPS + strip * 16 + strip_row * 2 + strip_col
    return jnp.where(west | east, side, inside)


def edge_slot(source, core):
    far = source - 9 * MESH
    other = ((far >> 8) + core) & 1
    coarse = COARSE_AT + other * 1024 + (far >> 9) * 256 + (far & 255)
    return jnp.where(far >= 0, coarse, near_slot(source, 0, NEAR_AT))


def kernel(
    grid, mesh_in, edge_in, g2m_src, g2m_dst, g2m_count, mesh_src, mesh_dst, m2g_src,
    weights_in, weights_out, gains, out,
    w, cells, table, edges, acc, pick, place, coarse, near, proj, message, mesh_now, own_part, strips, square,
    local_sem, send_sem, recv_sem,
):
    lat, lon = lax.axis_index("lat"), lax.axis_index("lon")
    z, core = lax.div(lat, 2), lax.rem(lat, 2)
    x, y = lax.div(lon, 4), lax.rem(lon, 4)
    counts = {"local": 0, "remote": 0}

    def local(src, dst):
        i = counts["local"]
        counts["local"] += 1
        copy = pltpu.make_async_copy(src, dst, local_sem.at[i])
        copy.start()
        return copy

    def remote(src, dst, device):
        i = counts["remote"]
        counts["remote"] += 1
        copy = pltpu.make_async_remote_copy(
            src_ref=src, dst_ref=dst, send_sem=send_sem.at[i], recv_sem=recv_sem.at[i],
            device_id=device, device_id_type=pl.DeviceIdType.MESH,
        )
        copy.start()
        return copy

    def beside(p, q):
        return (lax.rem(lat + (p + N_LAT), N_LAT), lax.rem(lon + (q + N_LON), N_LON))

    def chip(dx, dy, dz):
        return (lax.rem(z + dz, 4) * 2 + core, lax.rem(x + dx, 4) * 4 + lax.rem(y + dy, 4))

    sibling = (z * 2 + (1 - core), lon)

    got_grid = local(grid, cells.at[pl.ds(0, CELLS)])
    got_weights = []
    for first, many, first_out, many_out in ((0, 4, 0, 2), (4, 5, 2, 2), (9, 5, 4, 2), (14, 4, 6, 2)):
        got_weights.append((
            local(weights_in.at[pl.ds(first, many)], w.at[pl.ds(first, many)]),
            local(weights_out.at[pl.ds(first_out, many_out)], w.at[pl.ds(OUT + first_out, many_out)]),
        ))
        if first == 0:
            got_edges = local(edge_in, edges)

    barrier = pltpu.get_barrier_semaphore()
    peers = [beside(p, q) for p, q in NEIGHBOURS] + [chip(*d) for d in sorted(set(XY + YZ))] + [sibling]
    for peer in peers:
        pl.semaphore_signal(barrier, inc=1, device_id=peer, device_id_type=pl.DeviceIdType.MESH)

    got_grid.wait()
    i = lax.broadcasted_iota(jnp.int32, (16, COLS), 0)
    j = lax.broadcasted_iota(jnp.int32, (16, COLS), 1)
    for side, first, shift in ((0, COLS - 16, 14), (1, 0, 0)):
        rim = jnp.concatenate([cells[r * COLS + first : r * COLS + first + 16] for r in range(ROWS)], axis=0)
        wanted = (i >> 1) * 16 + shift + (i & 1)
        strips[side] = dot(ones_where(j == wanted), rim).astype(BF16)

    pl.semaphore_wait(barrier, len(peers))
    halo = [
        remote(grid.at[pl.ds(CELLS - 256, 256)], cells.at[pl.ds(CELLS, 256)], beside(1, 0)),
        remote(grid.at[pl.ds(0, 256)], cells.at[pl.ds(CELLS + 256, 256)], beside(-1, 0)),
    ]
    for side, q in ((0, 1), (1, -1)):
        for place_at, p in ((0, 0), (2, 1), (4, -1)):
            to = CELLS + 512 + (place_at + side) * 16
            halo.append(remote(strips.at[side], cells.at[pl.ds(to, 16)], beside(p, q)))

    lanes = lax.broadcasted_iota(jnp.int32, (128, 128), 1).astype(jnp.int16)
    nodes = lax.broadcasted_iota(jnp.int32, (MESH, 128), 0)

    def stacked(ref):
        square[...] = jnp.zeros_like(square)
        many = ref.shape[1] // 128
        for t in range(many):
            square[t : t + 1, :] = ref[0:1, t * 128 : t * 128 + 128].astype(F32)
        return square[...].astype(jnp.int32), many

    def columns(index, many, at):
        turned = index.astype(F32).T
        for t in range(many):
            acc[t * 128 : t * 128 + 128, at : at + 128] = jnp.broadcast_to(turned[:, t : t + 1], (128, 128))

    source, many = stacked(g2m_src)
    columns(grid_slot(source), many, 0)
    target, many = stacked(g2m_dst)
    columns(target + CELLS, many, 128)

    @pl.loop(0, G2M // 128)
    def _(t):
        rows = pl.ds(pl.multiple_of(t * 128, 128), 128)
        first, second = short(acc[rows, 0:128]), short(acc[rows, 128:256])
        for chunk in range(16):
            ids = lanes + jnp.int16(chunk * 128)
            mask = (second if 8 <= chunk < 11 else first) == ids
            pick[rows, chunk * 128 : chunk * 128 + 128] = ones_where_short(mask)

    live = g2m_count[...]
    lane = lax.broadcasted_iota(jnp.int32, (1, 128), 1)
    for t in range(G2M // 128):
        target = jnp.where(lane + t * 128 < live, g2m_dst[0:1, t * 128 : t * 128 + 128], -1)
        place[:, EDGE + t * 128 : EDGE + t * 128 + 128] = ones_where(nodes == target)

    got_weights[0][0].wait()
    got_weights[0][1].wait()

    @pl.loop(0, CELLS // TILE)
    def _(t):
        rows = pl.ds(pl.multiple_of(t * TILE, TILE), TILE)
        table[rows, :] = dot(cells[rows, :], w[0]).astype(BF16)

    table[CELLS : CELLS + MESH] = dot(mesh_in[...], w[1]).astype(BF16)
    table[CELLS + MESH : NORTH] = jnp.zeros((NORTH - CELLS - MESH, L), BF16)
    table[NORTH + 608 :] = jnp.zeros((2048 - NORTH - 608, L), BF16)
    own_part[...] = dot(mesh_in[...], w[2])

    @pl.loop(0, G2M // TILE)
    def _(t):
        rows = pl.ds(pl.multiple_of(t * TILE, TILE), TILE)
        acc[rows, :] = dot(pick[rows, 0:NORTH], table[0:NORTH])

    for copy in halo:
        copy.wait_recv()
    table[NORTH : NORTH + 608] = dot(cells[CELLS:GRID_ROWS], w[0]).astype(BF16)

    for rows in tiles(G2M):
        before = acc[rows, :] + dot(pick[rows, NORTH:2048], table[NORTH:2048])
        message[rows, :] = norm(dot(hidden(before), w[OUT]), gains[0:1, :]).astype(BF16)

    def new_nodes(old, self_part, totals, second, k):
        before = self_part + dot(totals.astype(BF16), w[second])
        return (old.astype(F32) + norm(dot(hidden(before), w[OUT + k]), gains[k : k + 1, :])).astype(BF16)

    def update_encoded(a, b):
        totals = dot(place[a:b, EDGE : EDGE + G2M], message[...])
        mesh_now[a:b] = new_nodes(mesh_in[a:b], own_part[a:b], totals, 3, 1)

    def update_round(r):
        def update(a, b):
            totals = dot(place[a:b, 0:EDGE], edges[...])
            mesh_now[a:b] = new_nodes(mesh_now[a:b], own_part[a:b], totals, 8 + 5 * r, 3 + 2 * r)

        return update

    sent = list(halo)

    def send_near(r):
        copies = []
        for slot, (p, q) in enumerate(NEIGHBOURS):
            copies.append(remote(proj.at[r, pl.ds(0, BORDER)], near.at[r, slot], beside(-p, -q)))
        sent.extend(copies)
        return copies

    def plane(r, part, axis, d):
        here = lax.rem({"x": x, "z": z}[axis] + (4 - d), 4)
        if axis == "z":
            return coarse.at[r, 0, here, :, :, :, part]
        return coarse.at[r, 0, :, here, :, :, part]

    update = update_encoded
    for r in range(ROUNDS):
        first = 4 + 5 * r
        got_weights[1 + r][0].wait()
        got_weights[1 + r][1].wait()
        update(MESH - COARSE, MESH)
        coarse[r, 0, z, x, y] = dot(mesh_now[MESH - COARSE : MESH], w[first + 1]).astype(BF16)
        arriving = []
        for part, axis, offsets in PARTS:
            ref = coarse.at[r, 0, z, x, y, :, part]
            arriving.append([remote(ref, ref, chip(*d)) for d in offsets])
            sent.extend(arriving[-1])
        update(0, MESH - COARSE)
        proj[r, 0:MESH] = dot(mesh_now[...], w[first + 1]).astype(BF16)
        got_near = send_near(r)
        proj[r, MESH : 2 * MESH] = dot(mesh_now[...], w[first + 2]).astype(BF16)
        own_part[...] = dot(mesh_now[...], w[first + 3])

        if r == 0:
            got_edges.wait()
            source, many = stacked(mesh_src)
            columns(edge_slot(source, core), many, 0)
            target, many = stacked(mesh_dst)
            columns(target + MESH, many, 128)

        across = []

        def second_stage():
            moving = []
            for k, (part, axis, offsets) in enumerate(PARTS):
                for copy in arriving[k]:
                    copy.wait_recv()
                ref = plane(r, part, axis, 0)
                moving.append([
                    remote(ref, ref, chip(**{"dx": 0, "dy": 0, "dz": 0, "d" + axis: d})) for d in (1, 2, 3)
                ])
                sent.extend(moving[-1])
            for part, axis, offsets in PARTS:
                across.append(forward(part, axis, 0))
            return moving

        def forward(part, axis, d):
            here = lax.rem({"x": x, "z": z}[axis] + (4 - d), 4)
            if axis == "z":
                return remote(
                    coarse.at[r, 0, here, :, :, :, part], coarse.at[r, 1, here, :, :, :, part], sibling
                )
            return remote(
                coarse.at[r, 0, :, here, :, :, part], coarse.at[r, 1, :, here, :, :, part], sibling
            )

        if r == 0:
            moving = second_stage()

            @pl.loop(0, EDGE // 128)
            def _(t):
                rows = pl.ds(pl.multiple_of(t * 128, 128), 128)
                one, two = short(acc[rows, 0:128]), short(acc[rows, 128:256])
                for chunk in range(WIDE // 128):
                    ids = lanes + jnp.int16(chunk * 128)
                    if chunk in (3, 4):
                        mask = two == ids
                    elif chunk == 2:
                        mask = (one == ids) | (two == ids)
                    else:
                        mask = one == ids
                    pick[rows, chunk * 128 : chunk * 128 + 128] = ones_where_short(mask)

            for t in range(EDGE // 128):
                place[:, t * 128 : t * 128 + 128] = ones_where(nodes == mesh_dst[0:1, t * 128 : t * 128 + 128])

        if r == 0:
            for copy in got_near:
                copy.wait_recv()
            for rows in tiles(EDGE):
                acc[rows, :] = (
                    dot(edges[rows, :], w[first])
                    + dot(pick[rows, 0:NEAR_AT], proj[r])
                    + dot(pick[rows, NEAR_AT:COARSE_AT], near[r].reshape(8 * BORDER, L))
                )
        else:
            for t, rows in enumerate(tiles(EDGE)):
                if t == 3:
                    moving = second_stage()
                acc[rows, :] = dot(edges[rows, :], w[first]) + dot(pick[rows, 0:NEAR_AT], proj[r])
            for copy in got_near:
                copy.wait_recv()
            for rows in tiles(EDGE):
                acc[rows, :] += dot(pick[rows, NEAR_AT:COARSE_AT], near[r].reshape(8 * BORDER, L))

        for d in (1, 2, 3):
            for k, (part, axis, offsets) in enumerate(PARTS):
                moving[k][d - 1].wait_recv()
                across.append(forward(part, axis, d))
        sent.extend(across)

        for rows in tiles(EDGE):
            acc[rows, :] += dot(pick[rows, COARSE_AT : COARSE_AT + 1024], coarse[r, 0].reshape(1024, L))

        for copy in across:
            copy.wait_recv()

        for rows in tiles(EDGE):
            before = acc[rows, :] + dot(pick[rows, COARSE_AT + 1024 : WIDE], coarse[r, 1].reshape(1024, L))
            result = norm(dot(hidden(before), w[OUT + 2 + 2 * r]), gains[2 + 2 * r : 3 + 2 * r, :])
            edges[rows, :] = (edges[rows, :].astype(F32) + result).astype(BF16)

        update = update_round(r)

    got_weights[3][0].wait()
    got_weights[3][1].wait()
    update(0, BORDER)
    proj[ROUNDS, 0:BORDER] = dot(mesh_now[0:BORDER], w[14]).astype(BF16)
    got_near = send_near(ROUNDS)
    update(BORDER, MESH)
    proj[ROUNDS, BORDER:MESH] = dot(mesh_now[BORDER:MESH], w[14]).astype(BF16)
    proj[ROUNDS, MESH : 2 * MESH] = jnp.zeros((MESH, L), BF16)

    square[...] = jnp.zeros_like(square)
    square[0:24] = m2g_src[...].astype(F32)
    columns(near_slot(square[...].astype(jnp.int32), 0, DEC_OWN), 24, 0)

    @pl.loop(0, ROWS)
    def _(t):
        to = pl.ds(pl.multiple_of(t * 128, 128), 128)
        for corner in range(3):
            one = short(acc[pl.ds(pl.multiple_of(corner * CELLS + t * 128, 128), 128), 0:128])
            for chunk in range(DEC_WIDE // 128):
                at = corner * DEC_WIDE + chunk * 128
                pick[to, at : at + 128] = ones_where_short(one == lanes + jnp.int16(chunk * 128))

    @pl.loop(0, CELLS // TILE)
    def _(t):
        rows = pl.ds(pl.multiple_of(t * TILE, TILE), TILE)
        base = dot(cells[rows, :], w[15])
        for corner in range(3):
            at = corner * DEC_WIDE
            to = pl.ds(pl.multiple_of(corner * CELLS + t * TILE, TILE), TILE)
            acc[to, :] = base + dot(pick[rows, at : at + DEC_OWN], proj[ROUNDS, 0:DEC_OWN])

    for copy in got_near:
        copy.wait_recv()

    @pl.loop(0, CELLS // TILE)
    def _(t):
        rows = pl.ds(pl.multiple_of(t * TILE, TILE), TILE)
        totals = jnp.zeros((TILE, L), F32)
        for corner in range(3):
            at = corner * DEC_WIDE
            to = pl.ds(pl.multiple_of(corner * CELLS + t * TILE, TILE), TILE)
            before = acc[to, :] + dot(
                pick[rows, at + DEC_OWN : at + DEC_WIDE], near[ROUNDS].reshape(8 * BORDER, L)
            )
            totals = totals + norm(dot(hidden(before), w[OUT + 6]), gains[6:7, :])
        out[rows, :] = new_nodes(cells[rows, :], dot(cells[rows, :], w[16]), totals, 17, 7)

    for copy in sent:
        copy.wait_send()


def on_device(
    grid_latent, mesh_latent, edge_latent, g2m_src, g2m_dst, g2m_count, mesh_src, mesh_dst, m2g_src,
    weights_in, weights_out, gains,
):
    anywhere = pl.BlockSpec(memory_space=pl.ANY)
    vmem = pl.BlockSpec(memory_space=pltpu.VMEM)
    result = pl.pallas_call(
        kernel,
        out_shape=jax.ShapeDtypeStruct((CELLS, L), BF16),
        in_specs=[anywhere, vmem, anywhere] + [vmem] * 6 + [anywhere, anywhere, vmem],
        out_specs=vmem,
        scratch_shapes=[
            pltpu.VMEM((26, L, L), BF16),
            pltpu.VMEM((GRID_ROWS, L), BF16),
            pltpu.VMEM((2048, L), BF16),
            pltpu.VMEM((EDGE, L), BF16),
            pltpu.VMEM((3 * CELLS, L), F32),
            pltpu.VMEM((EDGE, WIDE), BF16),
            pltpu.VMEM((MESH, EDGE + G2M), BF16),
            pltpu.VMEM((ROUNDS, 2, 4, 4, 4, COARSE, L), BF16),
            pltpu.VMEM((ROUNDS + 1, 8, BORDER, L), BF16),
            pltpu.VMEM((ROUNDS + 1, 2 * MESH, L), BF16),
            pltpu.VMEM((G2M, L), BF16),
            pltpu.VMEM((MESH, L), BF16),
            pltpu.VMEM((MESH, L), F32),
            pltpu.VMEM((2, 16, L), BF16),
            pltpu.VMEM((128, 128), F32),
            pltpu.SemaphoreType.DMA((10,)),
            pltpu.SemaphoreType.DMA((120,)),
            pltpu.SemaphoreType.DMA((120,)),
        ],
        compiler_params=pltpu.CompilerParams(
            collective_id=0, has_side_effects=True, vmem_limit_bytes=62 * 1024 * 1024
        ),
        cost_estimate=pl.CostEstimate(flops=40_000_000_000, bytes_accessed=20_000_000, transcendentals=10_000_000),
    )(
        grid_latent.reshape(CELLS, L), mesh_latent.reshape(MESH, L), edge_latent.reshape(EDGE, L),
        g2m_src.reshape(1, G2M), g2m_dst.reshape(1, G2M), g2m_count,
        mesh_src.reshape(1, EDGE), mesh_dst.reshape(1, EDGE), m2g_src.reshape(-1, 128),
        weights_in, weights_out, gains,
    )
    return result.reshape(grid_latent.shape)


def solution(mesh):
    placed = (
        P("lat", "lon", None),
        P("lat", "lon", None, None),
        P("lat", "lon", None, None),
        P("lat", "lon", None),
        P("lat", "lon", None),
        P("lat", "lon"),
        P("lat", "lon", None),
        P("lat", "lon", None),
        P(None, "lat", "lon"),
        P(),
        P(),
        P(),
    )
    return jax.shard_map(
        on_device, mesh=mesh, in_specs=placed, out_specs=P("lat", "lon", None), check_vma=False
    )
```
